768 devices in a mesh: atoms: 12 (over z), aux: 64 (over y, x, core).
Axes of the slice: x: 4, y: 8, z: 12, core: 2. Of those that a mesh axis runs over, the one named last changes fastest.
Arguments:
- coefficients: bfloat16 [768, 73728], P('atoms', 'aux'), may hold values from -6 to 6
- density: bfloat16 [72, 576], P('atoms'), may hold values from -1.25 to 1.25
- metric: float32 [72, 128, 128], P('atoms', 'aux')
- pair_atoms: int32 [72, 2], replicated, may hold values from 0 to 767, as said below
- home_row: int32 [768], replicated, may hold values from 0 to 767, as said below
Outputs:
- exchange_blocks: float32 [72, 576], P('atoms')
The draws below stay inside these ranges and needn't reach their ends.
Inputs may be any that keep to these rules, and one draw needn't show every extreme that they name: `pair_atoms`: pairs 6 d to 6 (d + 1) - 1 form group d. Of the 12 atoms that a group names (with repeats), at most 2 have home rows in any one range of 64 rows k * 64 to (k + 1) * 64 - 1, and in every group some range holds exactly 2. `home_row`: A permutation of the rows 0 to 767.
All inputs are finite; a program needn't handle non-finite values.
Results may differ from the reference program's by a relative error of at most 0.0003.
Values may be sent and summed in bfloat16 or wider, within the bound.
No kernel may reach another device: no remote copies, remote signals or barrier semaphores. Data moves between devices by JAX's collectives and lax.ppermute only.
A program may use at most 32 MiB of HBM per device.

```python
import math
import jax
import jax.numpy as jnp
from jax import lax

NB = 24
NA = 128
AT_DEV = 64
PAIR_DEV = 6
CAP = 2
ATOMS = 768
PAIRS = 72
N_ATOMS = 12


def shared_order(key):
    return jax.random.permutation(key, ATOMS).astype(jnp.int32)


def draw_home_row(key, part):
    order = shared_order(key)
    return order


def device_rows(key):
    keys = jax.random.split(key, 4)
    leading = jax.random.randint(keys[0], (), 0, N_ATOMS).astype(jnp.int32)
    others = (jnp.repeat(jnp.arange(1, N_ATOMS, dtype=jnp.int32), CAP) + leading) % N_ATOMS
    others = jax.random.permutation(keys[1], others)[:2 * PAIR_DEV - CAP]
    owners = jnp.concatenate([jnp.full((CAP,), leading, jnp.int32), others])
    owners = jax.random.permutation(keys[2], owners)
    within = jax.random.randint(keys[3], (2 * PAIR_DEV,), 0, AT_DEV).astype(jnp.int32)
    return owners * AT_DEV + within


def draw_pair_atoms(key, part):
    order = shared_order(key)
    key = jax.random.fold_in(key, 23)
    atom_at = jnp.zeros((ATOMS,), jnp.int32).at[order].set(jnp.arange(ATOMS, dtype=jnp.int32))
    rows = jax.vmap(device_rows)(jax.random.split(key, N_ATOMS))
    return atom_at[rows].reshape(PAIRS, 2)


def draw_metric(key, part):
    key = jax.random.fold_in(key, 37)
    keys = jax.random.split(key, 2)
    diagonal = jax.random.uniform(keys[0], (PAIRS, NA), jnp.float32, 1.0, 2.0)
    spread = jax.random.normal(keys[1], (PAIRS, NA, NA), jnp.float32)
    identity = jnp.eye(NA, dtype=jnp.float32)
    block = identity[None] * diagonal[:, :, None] + 0.5 / math.sqrt(NA) * spread
    return (block / math.sqrt(NA * NB)).astype(jnp.float32)


def block_levels(rng, shape, pieces, least, top_value):
    loudness = 1.0
    for dim, shards_of in pieces:
        steps = jax.random.uniform(jax.random.fold_in(jax.random.fold_in(rng, 6), dim), (shards_of,), jnp.float32, least / len(pieces), top_value / len(pieces))
        loudness = loudness * jnp.repeat(jnp.exp(steps), shape[dim] // shards_of).reshape((-1,) + (1,) * (len(shape) - 1 - dim))
    return loudness


def gaussian(rng, shape, scale, reach, pieces=(), kind=jnp.bfloat16):
    drawn = jax.random.normal(rng, shape, jnp.float32) * scale
    if len(pieces) > 0:
        drawn = block_levels(rng, shape, pieces, -0.22, 0.18) * drawn
    return jnp.clip(drawn, min=-reach, max=reach).astype(kind)


def setup_inputs(seed: int = 0) -> dict:
    streams_of = jax.random.split(jax.random.key(seed), 6)
    coefficients = gaussian(streams_of[0], (ATOMS, NA * NB * NB), 1.0, 6.0, ((0, 12), (1, 64)))
    density = gaussian(streams_of[1], (PAIRS, NB * NB), NB ** -0.5, 1.25, ((0, 12),))
    metric = draw_metric(jax.random.fold_in(streams_of[5], 71), 0)
    pair_atoms = draw_pair_atoms(jax.random.fold_in(streams_of[5], 71), 0)
    home_row = draw_home_row(jax.random.fold_in(streams_of[5], 71), 0)
    return dict(coefficients=coefficients, density=density, metric=metric, pair_atoms=pair_atoms, home_row=home_row)


def reference(coefficients, density, metric, pair_atoms, home_row):
    rows = home_row[pair_atoms]

    def pair_block(inputs):
        row_pair, density_row, metric_block = inputs
        first_side = coefficients[row_pair[0]].reshape(NA, NB, NB).astype(jnp.float32)
        second_side = coefficients[row_pair[1]].reshape(NA, NB, NB).astype(jnp.float32)
        density_block = density_row.reshape(NB, NB).astype(jnp.float32)
        projected = jnp.einsum("qmk,kl->qml", first_side, density_block, precision=lax.Precision.HIGHEST)
        weighted = jnp.einsum("qr,rnl->qnl", metric_block, second_side, precision=lax.Precision.HIGHEST)
        result = jnp.einsum("qml,qnl->mn", projected, weighted, precision=lax.Precision.HIGHEST)
        return result.reshape(NB * NB)

    return lax.map(pair_block, (rows, density, metric))
```

```python
import jax
import jax.numpy as jnp
from jax import lax
from jax.experimental import pallas as pl
from jax.experimental.pallas import tpu as pltpu
from jax.sharding import Mesh, PartitionSpec as P

NB = 24
BLOCK = NB * NB
SLOTS = 2
CORES = 2
CHIP_AXES = ("chip", "core")
BF16 = jnp.bfloat16
F32 = jnp.float32


def split_two(x):
    high = x.astype(BF16)
    return high, (x - high.astype(F32)).astype(BF16)


def match(shape, dim_a, div_a, dim_b, div_b, mod_a=None, mod_b=None):
    a = lax.broadcasted_iota(jnp.int32, shape, dim_a) // div_a
    b = lax.broadcasted_iota(jnp.int32, shape, dim_b) // div_b
    a = a if mod_a is None else a % mod_a
    b = b if mod_b is None else b % mod_b
    return a == b


def dot(a, b):
    return jnp.dot(a, b, preferred_element_type=F32)


def exchange_kernel(sides_ref, metric_ref, density_ref, out_ref):
    pairs = sides_ref.shape[0]
    spread = match((NB, BLOCK), 0, 1, 1, 1, mod_b=NB).astype(BF16)
    tops = []
    for t in range(pairs):
        first, second = sides_ref[t, 0], sides_ref[t, 1]
        mixed = dot(metric_ref[t, 0], second) + dot(metric_ref[t, 1], second)
        high, low = split_two(mixed)
        gram = lax.dot_general(
            jnp.concatenate([first, first], 0),
            jnp.concatenate([high, low], 0),
            (((0,), (0,)), ((), ())),
            preferred_element_type=F32,
        )
        weight = dot(density_ref[t], spread)
        tops.append(jnp.sum(gram.reshape(NB, NB, BLOCK) * weight[None], axis=1))
    top = jnp.concatenate(tops, 0)
    high, low = split_two(top)
    fold = match((BLOCK, BLOCK), 0, NB, 1, 1, mod_b=NB).astype(BF16)
    flat = dot(high, fold) + dot(low, fold)
    keep = match((pairs * NB, BLOCK), 0, 1, 1, NB, mod_a=NB)
    flat = jnp.where(keep, flat, 0.0).reshape(pairs, NB, BLOCK)
    out_ref[...] = jnp.sum(flat, axis=1)


def shards(coefficients, density, metric, pair_atoms, home_row):
    groups = lax.axis_size("atoms")
    sources = lax.axis_size(CHIP_AXES)
    me = lax.axis_index("atoms")
    core = lax.axis_index("core")
    stored, width = coefficients.shape
    pairs = density.shape[0]
    entries = 2 * pairs
    core_pairs = pairs // CORES
    local_aux = width // BLOCK
    all_aux = sources * local_aux

    wanted = home_row[pair_atoms].reshape(groups, entries)
    owner = wanted // stored
    earlier = jnp.arange(entries)[:, None] > jnp.arange(entries)[None, :]
    slot = jnp.sum((owner[:, :, None] == owner[:, None, :]) & earlier[None], axis=2)
    row = jnp.where((wanted // stored) == me, wanted % stored, -1)
    pick_out = (slot[:, None, :, None] == jnp.arange(SLOTS)[None, :, None, None]) & (
        row[:, None, :, None] == jnp.arange(stored)[None, None, None, :]
    )
    pick_out = jnp.any(pick_out, axis=2).astype(BF16).reshape(groups * SLOTS, stored)
    leaving = dot(pick_out, coefficients).astype(BF16).reshape(groups, SLOTS, width)
    arrived = lax.all_to_all(leaving, "atoms", 0, 0).reshape(groups * SLOTS, width)

    place = lax.dynamic_index_in_dim(owner * SLOTS + slot, me, 0, keepdims=False)
    pick_in = (place[:, None] == jnp.arange(groups * SLOTS)[None, :]).astype(BF16)
    rows = dot(pick_in, arrived).astype(BF16).reshape(CORES, core_pairs, 2, width)

    order = metric.reshape(pairs, local_aux, sources, local_aux).swapaxes(2, 3)
    order = order.reshape(pairs, local_aux * all_aux)
    coarse = lax.reduce_precision(order, 8, 7)
    metric_two = jnp.stack([coarse.astype(BF16), (order - coarse).astype(BF16)], axis=1)
    metric_two = metric_two.reshape(CORES, core_pairs, 2, local_aux * all_aux)
    message = jnp.concatenate([rows, metric_two], axis=3)
    message = jnp.broadcast_to(message[None], (sources // CORES,) + message.shape)
    message = message.reshape(sources, core_pairs, 2, -1)
    everyone = lax.all_to_all(message, CHIP_AXES, 0, 0)

    sides = everyone[..., :width].reshape(sources, core_pairs, 2, local_aux, BLOCK)
    sides = sides.transpose(1, 2, 3, 0, 4).reshape(core_pairs, 2, all_aux, BLOCK)
    terms = everyone[..., width:].reshape(sources, core_pairs, 2, local_aux, all_aux)
    terms = terms.transpose(1, 2, 3, 0, 4).reshape(core_pairs, 2, all_aux, all_aux)
    mine = lax.dynamic_slice_in_dim(density, core * core_pairs, core_pairs, 0)
    out = pl.pallas_call(
        exchange_kernel,
        out_shape=jax.ShapeDtypeStruct((core_pairs, BLOCK), F32),
        compiler_params=pltpu.CompilerParams(vmem_limit_bytes=32 * 2**20),
    )(sides, terms, mine.reshape(core_pairs, NB, NB))
    return lax.all_gather(out, "core", axis=0, tiled=True)


def solution(mesh):
    atoms, aux = mesh.devices.shape
    fine = Mesh(mesh.devices.reshape(atoms, aux // CORES, CORES), ("atoms",) + CHIP_AXES)
    placed = (P("atoms", CHIP_AXES), P("atoms", None), P("atoms", CHIP_AXES, None), P(), P())
    return jax.shard_map(
        shards, mesh=fine, in_specs=placed, out_specs=P("atoms", None), check_vma=False
    )
```

```python
import jax
import jax.numpy as jnp
from jax import lax
from jax.experimental import pallas as pl
from jax.experimental.pallas import tpu as pltpu
from jax.sharding import Mesh, PartitionSpec as P

NB = 24
BLOCK = NB * NB
SLOTS = 2
COLUMNS = 8
AUX_AXES = ("line", "column")
BF16 = jnp.bfloat16
F32 = jnp.float32


def split_two(x):
    high = x.astype(BF16)
    return high, (x - high.astype(F32)).astype(BF16)


def match(shape, dim_a, div_a, dim_b, div_b, mod_a=None, mod_b=None):
    a = lax.broadcasted_iota(jnp.int32, shape, dim_a) // div_a
    b = lax.broadcasted_iota(jnp.int32, shape, dim_b) // div_b
    a = a if mod_a is None else a % mod_a
    b = b if mod_b is None else b % mod_b
    return a == b


def dot(a, b):
    return jnp.dot(a, b, preferred_element_type=F32)


def exchange_kernel(sides_ref, metric_ref, density_ref, out_ref):
    first, second = sides_ref[0], sides_ref[1]
    mixed = dot(metric_ref[0], second) + dot(metric_ref[1], second)
    high, low = split_two(mixed)
    gram = lax.dot_general(
        jnp.concatenate([first, first], 0),
        jnp.concatenate([high, low], 0),
        (((0,), (0,)), ((), ())),
        preferred_element_type=F32,
    )
    spread = match((NB, BLOCK), 0, 1, 1, 1, mod_b=NB).astype(BF16)
    weight = dot(density_ref[...], spread)
    top = jnp.sum(gram.reshape(NB, NB, BLOCK) * weight[None], axis=1)
    high, low = split_two(top)
    fold = match((BLOCK, BLOCK), 0, NB, 1, 1, mod_b=NB).astype(BF16)
    flat = dot(high, fold) + dot(low, fold)
    keep = match((NB, BLOCK), 0, 1, 1, NB)
    flat = jnp.sum(jnp.where(keep, flat, 0.0), axis=0, keepdims=True)
    out_ref[...] = jnp.broadcast_to(flat[None], out_ref.shape)


def shards(coefficients, density, metric, pair_atoms, home_row):
    groups = lax.axis_size("atoms")
    columns = lax.axis_size("column")
    lines = lax.axis_size("line")
    sources = lines * columns
    me = lax.axis_index("atoms")
    stored, width = coefficients.shape
    pairs = density.shape[0]
    entries = 2 * pairs
    local_aux = width // BLOCK
    all_aux = sources * local_aux

    wanted = home_row[pair_atoms].reshape(groups, entries)
    owner = wanted // stored
    earlier = jnp.arange(entries)[:, None] > jnp.arange(entries)[None, :]
    slot = jnp.sum((owner[:, :, None] == owner[:, None, :]) & earlier[None], axis=2)
    row = jnp.where(owner == me, wanted % stored, -1)
    pick_out = (slot[:, None, :, None] == jnp.arange(SLOTS)[None, :, None, None]) & (
        row[:, None, :, None] == jnp.arange(stored)[None, None, None, :]
    )
    pick_out = jnp.any(pick_out, axis=2).astype(BF16).reshape(groups * SLOTS, stored)
    leaving = dot(pick_out, coefficients).astype(BF16).reshape(groups, SLOTS, width)
    arrived = lax.all_to_all(leaving, "atoms", 0, 0).reshape(groups * SLOTS, width)

    place = lax.dynamic_index_in_dim(owner * SLOTS + slot, me, 0, keepdims=False)
    pick_in = (place[:, None] == jnp.arange(groups * SLOTS)[None, :]).astype(BF16)
    rows = dot(pick_in, arrived).astype(BF16).reshape(pairs, 2, width)

    order = metric.reshape(pairs, local_aux, sources, local_aux).swapaxes(2, 3)
    order = order.reshape(pairs, local_aux * all_aux)
    coarse = lax.reduce_precision(order, 8, 7)
    metric_two = jnp.stack([coarse.astype(BF16), (order - coarse).astype(BF16)], axis=1)
    message = jnp.concatenate([rows, metric_two], axis=2)
    message = jnp.pad(message, ((0, columns - pairs), (0, 0), (0, 0)))
    message = jnp.broadcast_to(message[None], (lines,) + message.shape)
    message = message.reshape((sources,) + message.shape[2:])
    everyone = lax.all_to_all(message, AUX_AXES, 0, 0)

    sides = everyone[..., :width].reshape(sources, 2, local_aux, BLOCK)
    sides = sides.transpose(1, 2, 0, 3).reshape(2, all_aux, BLOCK)
    terms = everyone[..., width:].reshape(sources, 2, local_aux, all_aux)
    terms = terms.transpose(1, 2, 0, 3).reshape(2, all_aux, all_aux)
    mine = jnp.minimum(lax.axis_index("column"), pairs - 1)
    mine = lax.dynamic_index_in_dim(density, mine, 0, keepdims=False)
    out = pl.pallas_call(
        exchange_kernel,
        out_shape=jax.ShapeDtypeStruct((columns, 1, BLOCK), F32),
        compiler_params=pltpu.CompilerParams(vmem_limit_bytes=32 * 2**20),
    )(sides, terms, mine.reshape(NB, NB))
    return lax.all_to_all(out, "column", 0, 0)[:pairs, 0]


def solution(mesh):
    atoms, aux = mesh.devices.shape
    fine = Mesh(mesh.devices.reshape(atoms, aux // COLUMNS, COLUMNS), ("atoms",) + AUX_AXES)
    placed = (P("atoms", AUX_AXES), P("atoms", None), P("atoms", AUX_AXES, None), P(), P())
    return jax.shard_map(
        shards, mesh=fine, in_specs=placed, out_specs=P("atoms", None), check_vma=False
    )
```

```python
import jax
import jax.numpy as jnp
from jax import lax
from jax.experimental import pallas as pl
from jax.experimental.pallas import tpu as pltpu
from jax.sharding import Mesh, PartitionSpec as P

NB = 24
BLOCK = NB * NB
SLOTS = 2
ROWS, ACROSS, CORES = 2, 4, 2
COLUMN_AXES = ("row", "across")
CHIP_AXES = ("line",) + COLUMN_AXES
BF16 = jnp.bfloat16
F32 = jnp.float32


def split_two(x):
    high = x.astype(BF16)
    return high, (x - high.astype(F32)).astype(BF16)


def match(shape, dim_a, div_a, dim_b, div_b, mod_a=None, mod_b=None):
    a = lax.broadcasted_iota(jnp.int32, shape, dim_a) // div_a
    b = lax.broadcasted_iota(jnp.int32, shape, dim_b) // div_b
    a = a if mod_a is None else a % mod_a
    b = b if mod_b is None else b % mod_b
    return a == b


def dot(a, b):
    return jnp.dot(a, b, preferred_element_type=F32)


def exchange_kernel(own_ref, second_ref, density_ref, out_ref):
    count = own_ref.shape[0]
    half, width = count // 2, second_ref.shape[1]
    row = lax.broadcasted_iota(jnp.int32, (count, count), 0)
    column = lax.broadcasted_iota(jnp.int32, (count, count), 1)
    picked = jnp.where(row < half, 2 * row, 2 * (row - half) + 1) == column
    own = dot(picked.astype(BF16), own_ref[...]).astype(BF16)
    first = own[:half, :width]
    first = jnp.concatenate([first[:, :BLOCK], first[:, BLOCK:]], 0)
    terms = own[:, width:]
    aux = terms.shape[1] // 2
    high = jnp.concatenate([terms[:half, :aux], terms[:half, aux:]], 0)
    low = jnp.concatenate([terms[half:, :aux], terms[half:, aux:]], 0)
    second = second_ref[...]
    second = jnp.concatenate([second[:, :BLOCK], second[:, BLOCK:]], 0)
    mixed = dot(high, second) + dot(low, second)
    high, low = split_two(mixed)
    gram = lax.dot_general(
        jnp.concatenate([first, first], 0),
        jnp.concatenate([high, low], 0),
        (((0,), (0,)), ((), ())),
        preferred_element_type=F32,
    )
    spread = match((NB, BLOCK), 0, 1, 1, 1, mod_b=NB).astype(BF16)
    weight = dot(density_ref[...], spread)
    top = jnp.sum(gram.reshape(NB, NB, BLOCK) * weight[None], axis=1)
    high, low = split_two(top)
    fold = match((BLOCK, BLOCK), 0, NB, 1, 1, mod_b=NB).astype(BF16)
    flat = dot(high, fold) + dot(low, fold)
    keep = match((NB, BLOCK), 0, 1, 1, NB)
    flat = jnp.sum(jnp.where(keep, flat, 0.0), axis=0, keepdims=True)
    out_ref[...] = jnp.broadcast_to(flat[None], out_ref.shape)


def shards(coefficients, density, metric, pair_atoms, home_row):
    groups = lax.axis_size("atoms")
    columns = lax.axis_size(COLUMN_AXES)
    chips = lax.axis_size(CHIP_AXES)
    lines = chips // columns
    cores = lax.axis_size("core")
    me = lax.axis_index("atoms")
    stored, width = coefficients.shape
    pairs = density.shape[0]
    entries = 2 * pairs
    local_aux = width // BLOCK
    all_aux = chips * cores * local_aux

    wanted = home_row[pair_atoms].reshape(groups, entries)
    owner = wanted // stored
    earlier = jnp.arange(entries)[:, None] > jnp.arange(entries)[None, :]
    slot = jnp.sum((owner[:, :, None] == owner[:, None, :]) & earlier[None], axis=2)
    row = jnp.where(owner == me, wanted % stored, -1)
    pick_out = (slot[:, None, :, None] == jnp.arange(SLOTS)[None, :, None, None]) & (
        row[:, None, :, None] == jnp.arange(stored)[None, None, None, :]
    )
    pick_out = jnp.any(pick_out, axis=2).astype(BF16).reshape(groups * SLOTS, stored)
    leaving = dot(pick_out, coefficients).astype(BF16).reshape(groups, SLOTS, width)
    arrived = lax.all_to_all(leaving, "atoms", 0, 0).reshape(groups * SLOTS, width)

    place = lax.dynamic_index_in_dim(owner * SLOTS + slot, me, 0, keepdims=False)
    pick_in = (place[:, None] == jnp.arange(groups * SLOTS)[None, :]).astype(BF16)
    rows = dot(pick_in, arrived).astype(BF16).reshape(pairs, 2, width)

    order = metric.reshape(pairs, local_aux, chips, cores, local_aux)
    order = order.transpose(0, 1, 4, 3, 2).reshape(pairs, local_aux * all_aux)
    coarse = lax.reduce_precision(order, 8, 7)
    metric_two = jnp.stack([coarse.astype(BF16), (order - coarse).astype(BF16)], axis=1)
    message = jnp.concatenate([rows, metric_two], axis=2)
    message = jnp.pad(message, ((0, columns - pairs), (0, 0), (0, 0)))
    message = jnp.broadcast_to(message[None], (lines,) + message.shape)
    message = message.reshape((chips,) + message.shape[2:])
    everyone = lax.all_to_all(message, CHIP_AXES, 0, 0)

    second = lax.all_gather(everyone[:, 1, :width], "core", axis=0, tiled=True)
    mine = jnp.minimum(lax.axis_index(COLUMN_AXES), pairs - 1)
    mine = lax.dynamic_index_in_dim(density, mine, 0, keepdims=False)
    out = pl.pallas_call(
        exchange_kernel,
        out_shape=jax.ShapeDtypeStruct((columns * cores, 1, BLOCK), F32),
        compiler_params=pltpu.CompilerParams(vmem_limit_bytes=32 * 2**20),
    )(everyone.reshape(chips * 2, -1), second, mine.reshape(NB, NB))
    parts = lax.all_to_all(out, COLUMN_AXES + ("core",), 0, 0)
    return jnp.sum(parts.reshape(columns, cores, BLOCK), axis=1)[:pairs]


def solution(mesh):
    atoms, aux = mesh.devices.shape
    fine = mesh.devices.reshape(atoms, aux // (ROWS * ACROSS * CORES), ROWS, ACROSS, CORES)
    fine = Mesh(fine, ("atoms", "line", "row", "across", "core"))
    split = P("atoms", CHIP_AXES + ("core",))
    placed = (split, P("atoms", None), split, P(), P())
    return jax.shard_map(
        shards, mesh=fine, in_specs=placed, out_specs=P("atoms", None), check_vma=False
    )
```

```python
import jax
import jax.numpy as jnp
from jax import lax
from jax.experimental import pallas as pl
from jax.experimental.pallas import tpu as pltpu
from jax.sharding import Mesh, PartitionSpec as P

NB = 24
BLOCK = NB * NB
SLOTS = 2
ROWS, ACROSS, CORES = 2, 4, 2
COLUMNS = ROWS * ACROSS
LANES = 128
COLUMN_AXES = ("row", "across")
CHIP_AXES = ("line",) + COLUMN_AXES
BF16 = jnp.bfloat16
F32 = jnp.float32


def split_two(x):
    high = x.astype(BF16)
    return high, (x - high.astype(F32)).astype(BF16)


def match(shape, dim_a, div_a, dim_b, div_b, mod_a=None, mod_b=None):
    a = lax.broadcasted_iota(jnp.int32, shape, dim_a) // div_a
    b = lax.broadcasted_iota(jnp.int32, shape, dim_b) // div_b
    a = a if mod_a is None else a % mod_a
    b = b if mod_b is None else b % mod_b
    return a == b


def dot(a, b):
    return jnp.dot(a, b, preferred_element_type=F32)


def iota(shape, dim):
    return lax.broadcasted_iota(jnp.int32, shape, dim)


def leaving_kernel(me_ref, atoms_ref, home_ref, rows_ref, leaving_ref, pick_ref):
    me = me_ref[0].astype(F32)
    groups = leaving_ref.shape[0]
    stored = rows_ref.shape[0]
    chunks, lanes = home_ref.shape
    total = atoms_ref.shape[1]
    pairs = total // groups
    home = home_ref[...]
    owner_of = lax.div(home, stored).astype(F32).astype(BF16)
    within_of = lax.rem(home, stored).astype(F32).astype(BF16)
    square = (total, total)
    same = iota(square, 0) == iota(square, 1)
    before = iota(square, 0) < iota(square, 1)

    def column(x):
        return jnp.sum(jnp.where(same, x, 0.0), axis=1, keepdims=True)

    def count(condition):
        return jnp.sum(jnp.where(condition, 1.0, 0.0), axis=0, keepdims=True)

    group_row = lax.div(iota((1, total), 1), pairs).astype(F32)
    owner, within, key_row, key_column = [], [], [], []
    for side in range(2):
        atom = atoms_ref[side : side + 1, :]
        hit = (iota((lanes, total), 0) == lax.rem(atom, lanes)).astype(F32).astype(BF16)
        chunk = iota((chunks, total), 0) == lax.div(atom, lanes)
        owner.append(jnp.sum(jnp.where(chunk, dot(owner_of, hit), 0.0), axis=0, keepdims=True))
        within.append(jnp.sum(jnp.where(chunk, dot(within_of, hit), 0.0), axis=0, keepdims=True))
        key_row.append(group_row * groups + owner[side])
        key_column.append(column(key_row[side]))
    slot = [
        count((key_column[0] == key_row[0]) & before),
        count(key_column[0] == key_row[1]) + count((key_column[1] == key_row[1]) & before),
    ]
    sends = groups * SLOTS
    spots = (sends, total)
    dest = lax.div(iota(spots, 1), pairs) == lax.div(iota(spots, 0), SLOTS)
    turn = lax.rem(iota(spots, 0), SLOTS).astype(F32)
    entries = (2 * pairs, total)
    mine = iota(entries, 1) == me_ref[0] * pairs + lax.div(iota(entries, 0), 2)
    out, pick = 0.0, 0.0
    for side in range(2):
        chosen = dest & (slot[side] == turn) & (owner[side] == me)
        stored_at = column(within[side]).astype(jnp.int32) == iota((total, stored), 1)
        out += dot(chosen.astype(F32).astype(BF16), stored_at.astype(F32).astype(BF16))
        place = column(owner[side] * SLOTS + slot[side]).astype(jnp.int32)
        arrives = place == iota((total, sends), 1)
        local = mine & (lax.rem(iota(entries, 0), 2) == side)
        pick += dot(local.astype(F32).astype(BF16), arrives.astype(F32).astype(BF16))
    leaving = dot(out.astype(BF16), rows_ref[...]).astype(BF16)
    leaving_ref[...] = leaving.reshape(leaving_ref.shape)
    pick_ref[...] = pick.astype(BF16)


def message_kernel(arrived_ref, pick_ref, metric_ref, message_ref):
    pairs = metric_ref.shape[0] // 2
    chips = message_ref.shape[0]
    arrived = arrived_ref[...].reshape(pick_ref.shape[1], arrived_ref.shape[2])
    rows = dot(pick_ref[...], arrived).astype(BF16)
    rows = jnp.concatenate([rows, metric_ref[...]], axis=1).reshape(pairs, 2, -1)
    empty = jnp.zeros((COLUMNS - pairs,) + rows.shape[1:], BF16)
    for line in range(0, chips, COLUMNS):
        message_ref[line : line + pairs] = rows
        message_ref[line + pairs : line + COLUMNS] = empty


def exchange_kernel(own_ref, second_ref, density_ref, out_ref):
    count = own_ref.shape[0]
    half, width = count // 2, second_ref.shape[1]
    row = lax.broadcasted_iota(jnp.int32, (count, count), 0)
    column = lax.broadcasted_iota(jnp.int32, (count, count), 1)
    picked = jnp.where(row < half, 2 * row, 2 * (row - half) + 1) == column
    own = dot(picked.astype(BF16), own_ref[...]).astype(BF16)
    first = own[:half, :width]
    first = jnp.concatenate([first[:, :BLOCK], first[:, BLOCK:]], 0)
    terms = own[:, width:]
    aux = terms.shape[1] // 2
    high = jnp.concatenate([terms[:half, :aux], terms[:half, aux:]], 0)
    low = jnp.concatenate([terms[half:, :aux], terms[half:, aux:]], 0)
    second = second_ref[...]
    second = jnp.concatenate([second[:, :BLOCK], second[:, BLOCK:]], 0)
    mixed = dot(high, second) + dot(low, second)
    high, low = split_two(mixed)
    gram = lax.dot_general(
        jnp.concatenate([first, first], 0),
        jnp.concatenate([high, low], 0),
        (((0,), (0,)), ((), ())),
        preferred_element_type=F32,
    )
    spread = match((NB, BLOCK), 0, 1, 1, 1, mod_b=NB).astype(BF16)
    weight = dot(density_ref[...], spread)
    top = jnp.sum(gram.reshape(NB, NB, BLOCK) * weight[None], axis=1)
    high, low = split_two(top)
    fold = match((BLOCK, BLOCK), 0, NB, 1, 1, mod_b=NB).astype(BF16)
    flat = dot(high, fold) + dot(low, fold)
    keep = match((NB, BLOCK), 0, 1, 1, NB)
    flat = jnp.sum(jnp.where(keep, flat, 0.0), axis=0, keepdims=True)
    out_ref[...] = jnp.broadcast_to(flat[None], out_ref.shape)


def shards(coefficients, density, metric, pair_atoms, home_row):
    groups = lax.axis_size("atoms")
    columns = lax.axis_size(COLUMN_AXES)
    chips = lax.axis_size(CHIP_AXES)
    cores = lax.axis_size("core")
    me = lax.axis_index("atoms")
    width = coefficients.shape[1]
    pairs = density.shape[0]
    entries = 2 * pairs
    local_aux = width // BLOCK
    all_aux = chips * cores * local_aux

    in_smem = pl.BlockSpec(memory_space=pltpu.SMEM)
    in_vmem = pl.BlockSpec(memory_space=pltpu.VMEM)
    leaving, pick = pl.pallas_call(
        leaving_kernel,
        in_specs=[in_smem, in_vmem, in_vmem, in_vmem],
        out_specs=[in_vmem, in_vmem],
        out_shape=[
            jax.ShapeDtypeStruct((groups, SLOTS, width), BF16),
            jax.ShapeDtypeStruct((entries, groups * SLOTS), BF16),
        ],
    )(me.reshape(1), pair_atoms.T, home_row.reshape(-1, LANES), coefficients)
    arrived = lax.all_to_all(leaving, "atoms", 0, 0)

    order = metric.reshape(pairs, local_aux, chips, cores, local_aux)
    order = order.transpose(0, 1, 4, 3, 2).reshape(pairs, local_aux * all_aux)
    coarse = lax.reduce_precision(order, 8, 7)
    metric_two = jnp.stack([coarse.astype(BF16), (order - coarse).astype(BF16)], axis=1)
    metric_two = metric_two.reshape(entries, local_aux * all_aux)
    message = pl.pallas_call(
        message_kernel,
        in_specs=[in_vmem, in_vmem, in_vmem],
        out_specs=in_vmem,
        out_shape=jax.ShapeDtypeStruct((chips, 2, width + local_aux * all_aux), BF16),
    )(arrived, pick, metric_two)
    everyone = lax.all_to_all(message, CHIP_AXES, 0, 0)

    second = lax.all_gather(everyone[:, 1, :width], "core", axis=0, tiled=True)
    mine = jnp.minimum(lax.axis_index(COLUMN_AXES), pairs - 1)
    mine = lax.dynamic_index_in_dim(density, mine, 0, keepdims=False)
    out = pl.pallas_call(
        exchange_kernel,
        out_shape=jax.ShapeDtypeStruct((columns * cores, 1, BLOCK), F32),
        compiler_params=pltpu.CompilerParams(vmem_limit_bytes=32 * 2**20),
    )(everyone.reshape(chips * 2, -1), second, mine.reshape(NB, NB))
    parts = lax.all_to_all(out, COLUMN_AXES + ("core",), 0, 0)
    return jnp.sum(parts.reshape(columns, cores, BLOCK), axis=1)[:pairs]


def solution(mesh):
    atoms, aux = mesh.devices.shape
    fine = mesh.devices.reshape(atoms, aux // (ROWS * ACROSS * CORES), ROWS, ACROSS, CORES)
    fine = Mesh(fine, ("atoms", "line", "row", "across", "core"))
    split = P("atoms", CHIP_AXES + ("core",))
    placed = (split, P("atoms", None), split, P(), P())
    return jax.shard_map(
        shards, mesh=fine, in_specs=placed, out_specs=P("atoms", None), check_vma=False
    )
```

```python
import jax
import jax.numpy as jnp
from jax import lax
from jax.experimental import pallas as pl
from jax.experimental.pallas import tpu as pltpu
from jax.sharding import Mesh, PartitionSpec as P

NB = 24
BLOCK = NB * NB
SLOTS = 2
ROWS, ACROSS, CORES = 2, 4, 2
COLUMNS = ROWS * ACROSS
LANES = 128
COLUMN_AXES = ("row", "across")
CHIP_AXES = ("line",) + COLUMN_AXES
BF16 = jnp.bfloat16
F32 = jnp.float32
SMALL = pltpu.CompilerParams(vmem_limit_bytes=4 * 2**20)
LARGE = pltpu.CompilerParams(vmem_limit_bytes=16 * 2**20)


def split_two(x):
    high = x.astype(BF16)
    return high, (x - high.astype(F32)).astype(BF16)


def match(shape, dim_a, div_a, dim_b, div_b, mod_a=None, mod_b=None):
    a = lax.broadcasted_iota(jnp.int32, shape, dim_a) // div_a
    b = lax.broadcasted_iota(jnp.int32, shape, dim_b) // div_b
    a = a if mod_a is None else a % mod_a
    b = b if mod_b is None else b % mod_b
    return a == b


def dot(a, b):
    return jnp.dot(a, b, preferred_element_type=F32)


def iota(shape, dim):
    return lax.broadcasted_iota(jnp.int32, shape, dim)


def leaving_kernel(me_ref, atoms_ref, home_ref, rows_ref, leaving_ref, pick_ref):
    me = me_ref[0].astype(F32)
    groups = leaving_ref.shape[0]
    stored = rows_ref.shape[0]
    chunks, lanes = home_ref.shape
    total = atoms_ref.shape[1]
    pairs = total // groups
    home = home_ref[...]
    owner_of = lax.div(home, stored).astype(F32).astype(BF16)
    within_of = lax.rem(home, stored).astype(F32).astype(BF16)
    square = (total, total)
    same = iota(square, 0) == iota(square, 1)
    before = iota(square, 0) < iota(square, 1)

    def column(x):
        return jnp.sum(jnp.where(same, x, 0.0), axis=1, keepdims=True)

    def count(condition):
        return jnp.sum(jnp.where(condition, 1.0, 0.0), axis=0, keepdims=True)

    group_row = lax.div(iota((1, total), 1), pairs).astype(F32)
    owner, within, key_row, key_column = [], [], [], []
    for side in range(2):
        atom = atoms_ref[side : side + 1, :]
        hit = (iota((lanes, total), 0) == lax.rem(atom, lanes)).astype(F32).astype(BF16)
        chunk = iota((chunks, total), 0) == lax.div(atom, lanes)
        owner.append(jnp.sum(jnp.where(chunk, dot(owner_of, hit), 0.0), axis=0, keepdims=True))
        within.append(jnp.sum(jnp.where(chunk, dot(within_of, hit), 0.0), axis=0, keepdims=True))
        key_row.append(group_row * groups + owner[side])
        key_column.append(column(key_row[side]))
    slot = [
        count((key_column[0] == key_row[0]) & before),
        count(key_column[0] == key_row[1]) + count((key_column[1] == key_row[1]) & before),
    ]
    sends = groups * SLOTS
    spots = (sends, total)
    dest = lax.div(iota(spots, 1), pairs) == lax.div(iota(spots, 0), SLOTS)
    turn = lax.rem(iota(spots, 0), SLOTS).astype(F32)
    entries = (2 * pairs, total)
    mine = iota(entries, 1) == me_ref[0] * pairs + lax.div(iota(entries, 0), 2)
    out, pick = 0.0, 0.0
    for side in range(2):
        chosen = dest & (slot[side] == turn) & (owner[side] == me)
        stored_at = column(within[side]).astype(jnp.int32) == iota((total, stored), 1)
        out += dot(chosen.astype(F32).astype(BF16), stored_at.astype(F32).astype(BF16))
        place = column(owner[side] * SLOTS + slot[side]).astype(jnp.int32)
        arrives = place == iota((total, sends), 1)
        local = mine & (lax.rem(iota(entries, 0), 2) == side)
        pick += dot(local.astype(F32).astype(BF16), arrives.astype(F32).astype(BF16))
    leaving = dot(out.astype(BF16), rows_ref[...]).astype(BF16)
    leaving_ref[...] = leaving.reshape(leaving_ref.shape)
    pick_ref[...] = pick.astype(BF16)


def message_kernel(arrived_ref, pick_ref, metric_ref, message_ref):
    pairs = metric_ref.shape[0] // 2
    chips = message_ref.shape[0]
    arrived = arrived_ref[...].reshape(pick_ref.shape[1], arrived_ref.shape[2])
    rows = dot(pick_ref[...], arrived).astype(BF16)
    rows = jnp.concatenate([rows, metric_ref[...]], axis=1).reshape(pairs, 2, -1)
    empty = jnp.zeros((COLUMNS - pairs,) + rows.shape[1:], BF16)
    for line in range(0, chips, COLUMNS):
        message_ref[line : line + pairs] = rows
        message_ref[line + pairs : line + COLUMNS] = empty


def exchange_kernel(own_ref, second_ref, density_ref, out_ref):
    count = own_ref.shape[0]
    half, width = count // 2, second_ref.shape[1]
    row = lax.broadcasted_iota(jnp.int32, (count, count), 0)
    column = lax.broadcasted_iota(jnp.int32, (count, count), 1)
    picked = jnp.where(row < half, 2 * row, 2 * (row - half) + 1) == column
    own = dot(picked.astype(BF16), own_ref[...]).astype(BF16)
    first = own[:half, :width]
    first = jnp.concatenate([first[:, :BLOCK], first[:, BLOCK:]], 0)
    terms = own[:, width:]
    aux = terms.shape[1] // 2
    high = jnp.concatenate([terms[:half, :aux], terms[:half, aux:]], 0)
    low = jnp.concatenate([terms[half:, :aux], terms[half:, aux:]], 0)
    second = second_ref[...]
    second = jnp.concatenate([second[:, :BLOCK], second[:, BLOCK:]], 0)
    mixed = dot(high, second) + dot(low, second)
    high, low = split_two(mixed)
    gram = lax.dot_general(
        jnp.concatenate([first, first], 0),
        jnp.concatenate([high, low], 0),
        (((0,), (0,)), ((), ())),
        preferred_element_type=F32,
    )
    spread = match((NB, BLOCK), 0, 1, 1, 1, mod_b=NB).astype(BF16)
    weight = dot(density_ref[...], spread)
    top = jnp.sum(gram.reshape(NB, NB, BLOCK) * weight[None], axis=1)
    high, low = split_two(top)
    fold = match((BLOCK, BLOCK), 0, NB, 1, 1, mod_b=NB).astype(BF16)
    flat = dot(high, fold) + dot(low, fold)
    keep = match((NB, BLOCK), 0, 1, 1, NB)
    flat = jnp.sum(jnp.where(keep, flat, 0.0), axis=0, keepdims=True)
    out_ref[...] = jnp.broadcast_to(flat[None], out_ref.shape)


def shards(coefficients, density, metric, pair_atoms, home_row):
    groups = lax.axis_size("atoms")
    columns = lax.axis_size(COLUMN_AXES)
    chips = lax.axis_size(CHIP_AXES)
    cores = lax.axis_size("core")
    me = lax.axis_index("atoms")
    width = coefficients.shape[1]
    pairs = density.shape[0]
    entries = 2 * pairs
    local_aux = width // BLOCK
    all_aux = chips * cores * local_aux

    in_smem = pl.BlockSpec(memory_space=pltpu.SMEM)
    in_vmem = pl.BlockSpec(memory_space=pltpu.VMEM)
    leaving, pick = pl.pallas_call(
        leaving_kernel,
        in_specs=[in_smem, in_vmem, in_vmem, in_vmem],
        out_specs=[in_vmem, in_vmem],
        out_shape=[
            jax.ShapeDtypeStruct((groups, SLOTS, width), BF16),
            jax.ShapeDtypeStruct((entries, groups * SLOTS), BF16),
        ],
        compiler_params=SMALL,
    )(me.reshape(1), pair_atoms.T, home_row.reshape(-1, LANES), coefficients)
    arrived = lax.all_to_all(leaving, "atoms", 0, 0)

    order = metric.reshape(pairs, local_aux, chips, cores, local_aux)
    order = order.transpose(0, 1, 4, 3, 2).reshape(pairs, local_aux * all_aux)
    coarse = lax.reduce_precision(order, 8, 7)
    metric_two = jnp.stack([coarse.astype(BF16), (order - coarse).astype(BF16)], axis=1)
    metric_two = metric_two.reshape(entries, local_aux * all_aux)
    message = pl.pallas_call(
        message_kernel,
        in_specs=[in_vmem, in_vmem, in_vmem],
        out_specs=in_vmem,
        out_shape=jax.ShapeDtypeStruct((chips, 2, width + local_aux * all_aux), BF16),
        compiler_params=SMALL,
    )(arrived, pick, metric_two)
    everyone = lax.all_to_all(message, CHIP_AXES, 0, 0)

    second = lax.all_gather(everyone[:, 1, :width], "core", axis=0, tiled=True)
    mine = jnp.minimum(lax.axis_index(COLUMN_AXES), pairs - 1)
    mine = lax.dynamic_index_in_dim(density, mine, 0, keepdims=False)
    out = pl.pallas_call(
        exchange_kernel,
        out_shape=jax.ShapeDtypeStruct((columns * cores, 1, BLOCK), F32),
        compiler_params=LARGE,
    )(everyone.reshape(chips * 2, -1), second, mine.reshape(NB, NB))
    parts = lax.all_to_all(out, COLUMN_AXES + ("core",), 0, 0)
    return jnp.sum(parts.reshape(columns, cores, BLOCK), axis=1)[:pairs]


def solution(mesh):
    atoms, aux = mesh.devices.shape
    fine = mesh.devices.reshape(atoms, aux // (ROWS * ACROSS * CORES), ROWS, ACROSS, CORES)
    fine = Mesh(fine, ("atoms", "line", "row", "across", "core"))
    split = P("atoms", CHIP_AXES + ("core",))
    placed = (split, P("atoms", None), split, P(), P())
    return jax.shard_map(
        shards, mesh=fine, in_specs=placed, out_specs=P("atoms", None), check_vma=False
    )
```

```python
import jax
import jax.numpy as jnp
from jax import lax
from jax.experimental import pallas as pl
from jax.experimental.pallas import tpu as pltpu
from jax.sharding import Mesh, PartitionSpec as P

NB = 24
BLOCK = NB * NB
SLOTS = 2
ROWS, ACROSS, CORES = 2, 4, 2
COLUMNS = ROWS * ACROSS
LANES = 128
COLUMN_AXES = ("row", "across")
CHIP_AXES = ("line",) + COLUMN_AXES
BF16 = jnp.bfloat16
F32 = jnp.float32
SMALL = pltpu.CompilerParams(vmem_limit_bytes=4 * 2**20)
LARGE = pltpu.CompilerParams(vmem_limit_bytes=16 * 2**20)


def split_two(x):
    high = x.astype(BF16)
    return high, (x - high.astype(F32)).astype(BF16)


def match(shape, dim_a, div_a, dim_b, div_b, mod_a=None, mod_b=None):
    a = lax.broadcasted_iota(jnp.int32, shape, dim_a) // div_a
    b = lax.broadcasted_iota(jnp.int32, shape, dim_b) // div_b
    a = a if mod_a is None else a % mod_a
    b = b if mod_b is None else b % mod_b
    return a == b


def dot(a, b):
    return jnp.dot(a, b, preferred_element_type=F32)


def iota(shape, dim):
    return lax.broadcasted_iota(jnp.int32, shape, dim)


def one_hot(condition):
    return condition.astype(F32).astype(BF16)


def leaving_kernel(atoms_hbm, home_hbm, metric_hbm, rows_hbm, leaving_ref, pick_ref, terms_ref, atoms_ref, home_ref, metric_ref, rows_ref, sems):
    fetches = [
        pltpu.make_async_copy(source, target, sems.at[i])
        for i, (source, target) in enumerate(
            [(atoms_hbm, atoms_ref), (home_hbm, home_ref), (metric_hbm, metric_ref), (rows_hbm, rows_ref)]
        )
    ]
    for fetch in fetches:
        fetch.start()
    me = lax.axis_index("atoms")
    groups = leaving_ref.shape[0]
    stored = rows_ref.shape[0]
    chunks, lanes = home_ref.shape
    total = atoms_ref.shape[1]
    pairs = total // groups
    fetches[0].wait()
    fetches[1].wait()
    home = home_ref[...]
    owner_of = lax.div(home, stored).astype(F32).astype(BF16)
    within_of = lax.rem(home, stored).astype(F32).astype(BF16)
    square = (total, total)
    same = iota(square, 0) == iota(square, 1)
    before = iota(square, 0) < iota(square, 1)

    def column(x):
        return jnp.sum(jnp.where(same, x, 0.0), axis=1, keepdims=True)

    def count(condition):
        return jnp.sum(jnp.where(condition, 1.0, 0.0), axis=0, keepdims=True)

    group_row = lax.div(iota((1, total), 1), pairs).astype(F32)
    owner, within, key_row, key_column = [], [], [], []
    for side in range(2):
        atom = atoms_ref[side : side + 1, :]
        hit = one_hot(iota((lanes, total), 0) == lax.rem(atom, lanes))
        chunk = iota((chunks, total), 0) == lax.div(atom, lanes)
        owner.append(jnp.sum(jnp.where(chunk, dot(owner_of, hit), 0.0), axis=0, keepdims=True))
        within.append(jnp.sum(jnp.where(chunk, dot(within_of, hit), 0.0), axis=0, keepdims=True))
        key_row.append(group_row * groups + owner[side])
        key_column.append(column(key_row[side]))
    slot = [
        count((key_column[0] == key_row[0]) & before),
        count(key_column[0] == key_row[1]) + count((key_column[1] == key_row[1]) & before),
    ]
    sends = groups * SLOTS
    spots = (sends, total)
    dest = lax.div(iota(spots, 1), pairs) == lax.div(iota(spots, 0), SLOTS)
    turn = lax.rem(iota(spots, 0), SLOTS).astype(F32)
    entries = (2 * pairs, total)
    mine = iota(entries, 1) == me * pairs + lax.div(iota(entries, 0), 2)
    out, pick = 0.0, 0.0
    for side in range(2):
        chosen = dest & (slot[side] == turn) & (owner[side] == me.astype(F32))
        stored_at = column(within[side]).astype(jnp.int32) == iota((total, stored), 1)
        out += dot(one_hot(chosen), one_hot(stored_at))
        place = column(owner[side] * SLOTS + slot[side]).astype(jnp.int32)
        arrives = place == iota((total, sends), 1)
        local = mine & (lax.rem(iota(entries, 0), 2) == side)
        pick += dot(one_hot(local), one_hot(arrives))
    pick_ref[...] = pick.astype(BF16)
    fetches[2].wait()
    local_aux, all_aux = metric_ref.shape[1:]
    square = (all_aux, all_aux)
    chips = all_aux // (CORES * local_aux)
    core = lax.rem(lax.div(iota(square, 0), local_aux), CORES)
    target = lax.rem(iota(square, 0), local_aux) * CORES + core
    target = target * chips + lax.div(iota(square, 0), CORES * local_aux)
    order = one_hot(target == iota(square, 1))
    twice = (2 * pairs, pairs)
    owns = lax.div(iota(twice, 0), 2) == iota(twice, 1)
    term = lax.rem(iota(twice, 0), 2)
    for q in range(local_aux):
        high, low = split_two(metric_ref[:, q, :])
        both = dot(one_hot(owns & (term == 0)), high) + dot(one_hot(owns & (term == 1)), low)
        both = dot(both.astype(BF16), order).astype(BF16)
        terms_ref[:, q * all_aux : (q + 1) * all_aux] = both
    fetches[3].wait()
    leaving = dot(out.astype(BF16), rows_ref[...]).astype(BF16)
    leaving_ref[...] = leaving.reshape(leaving_ref.shape)


def message_kernel(arrived_ref, pick_ref, metric_ref, message_ref):
    pairs = metric_ref.shape[0] // 2
    chips = message_ref.shape[0]
    arrived = arrived_ref[...].reshape(pick_ref.shape[1], arrived_ref.shape[2])
    rows = dot(pick_ref[...], arrived).astype(BF16)
    rows = jnp.concatenate([rows, metric_ref[...]], axis=1).reshape(pairs, 2, -1)
    empty = jnp.zeros((COLUMNS - pairs,) + rows.shape[1:], BF16)
    for line in range(0, chips, COLUMNS):
        message_ref[line : line + pairs] = rows
        message_ref[line + pairs : line + COLUMNS] = empty


def exchange_kernel(own_ref, second_ref, density_ref, out_ref):
    count = own_ref.shape[0]
    half, width = count // 2, second_ref.shape[1]
    row = lax.broadcasted_iota(jnp.int32, (count, count), 0)
    column = lax.broadcasted_iota(jnp.int32, (count, count), 1)
    picked = jnp.where(row < half, 2 * row, 2 * (row - half) + 1) == column
    own = dot(picked.astype(BF16), own_ref[...]).astype(BF16)
    first = own[:half, :width]
    first = jnp.concatenate([first[:, :BLOCK], first[:, BLOCK:]], 0)
    terms = own[:, width:]
    aux = terms.shape[1] // 2
    high = jnp.concatenate([terms[:half, :aux], terms[:half, aux:]], 0)
    low = jnp.concatenate([terms[half:, :aux], terms[half:, aux:]], 0)
    second = second_ref[...]
    second = jnp.concatenate([second[:, :BLOCK], second[:, BLOCK:]], 0)
    mixed = dot(high, second) + dot(low, second)
    high, low = split_two(mixed)
    gram = lax.dot_general(
        jnp.concatenate([first, first], 0),
        jnp.concatenate([high, low], 0),
        (((0,), (0,)), ((), ())),
        preferred_element_type=F32,
    )
    pairs = density_ref.shape[0]
    mine = lax.axis_index("row") * ACROSS + lax.axis_index("across")
    mine = iota((pairs, 1), 0) == jnp.minimum(mine, pairs - 1)
    block = jnp.sum(jnp.where(mine, density_ref[...].astype(F32), 0.0), axis=0, keepdims=True)
    block = jnp.where(match((NB, BLOCK), 0, 1, 1, NB), block, 0.0).astype(BF16)
    block = dot(block, match((BLOCK, NB), 0, 1, 1, 1, mod_a=NB).astype(BF16)).astype(BF16)
    spread = match((NB, BLOCK), 0, 1, 1, 1, mod_b=NB).astype(BF16)
    weight = dot(block, spread)
    top = jnp.sum(gram.reshape(NB, NB, BLOCK) * weight[None], axis=1)
    high, low = split_two(top)
    fold = match((BLOCK, BLOCK), 0, NB, 1, 1, mod_b=NB).astype(BF16)
    flat = dot(high, fold) + dot(low, fold)
    keep = match((NB, BLOCK), 0, 1, 1, NB)
    flat = jnp.sum(jnp.where(keep, flat, 0.0), axis=0, keepdims=True)
    out_ref[...] = jnp.broadcast_to(flat[None], out_ref.shape)


def shards(coefficients, density, metric, pair_atoms, home_row):
    groups = lax.axis_size("atoms")
    columns = lax.axis_size(COLUMN_AXES)
    chips = lax.axis_size(CHIP_AXES)
    cores = lax.axis_size("core")
    width = coefficients.shape[1]
    pairs = density.shape[0]
    entries = 2 * pairs
    local_aux = width // BLOCK
    all_aux = chips * cores * local_aux

    in_hbm = pl.BlockSpec(memory_space=pltpu.HBM)
    in_vmem = pl.BlockSpec(memory_space=pltpu.VMEM)
    sources = [pair_atoms.T, home_row.reshape(-1, LANES), metric, coefficients]
    leaving, pick, terms = pl.pallas_call(
        leaving_kernel,
        in_specs=[in_hbm] * 4,
        out_specs=[in_vmem] * 3,
        out_shape=[
            jax.ShapeDtypeStruct((groups, SLOTS, width), BF16),
            jax.ShapeDtypeStruct((entries, groups * SLOTS), BF16),
            jax.ShapeDtypeStruct((entries, local_aux * all_aux), BF16),
        ],
        scratch_shapes=[pltpu.VMEM(x.shape, x.dtype) for x in sources] + [pltpu.SemaphoreType.DMA((4,))],
        compiler_params=SMALL,
    )(*sources)
    arrived = lax.all_to_all(leaving, "atoms", 0, 0)

    message = pl.pallas_call(
        message_kernel,
        in_specs=[in_vmem, in_vmem, in_vmem],
        out_specs=in_vmem,
        out_shape=jax.ShapeDtypeStruct((chips, 2, width + local_aux * all_aux), BF16),
        compiler_params=SMALL,
    )(arrived, pick, terms)
    everyone = lax.all_to_all(message, CHIP_AXES, 0, 0)

    second = lax.all_gather(everyone[:, 1, :width], "core", axis=0, tiled=True)
    out = pl.pallas_call(
        exchange_kernel,
        out_shape=jax.ShapeDtypeStruct((columns * cores, 1, BLOCK), F32),
        compiler_params=LARGE,
    )(everyone.reshape(chips * 2, -1), second, density)
    parts = lax.all_to_all(out, COLUMN_AXES + ("core",), 0, 0)
    return jnp.sum(parts.reshape(columns, cores, BLOCK), axis=1)[:pairs]


def solution(mesh):
    atoms, aux = mesh.devices.shape
    fine = mesh.devices.reshape(atoms, aux // (ROWS * ACROSS * CORES), ROWS, ACROSS, CORES)
    fine = Mesh(fine, ("atoms", "line", "row", "across", "core"))
    split = P("atoms", CHIP_AXES + ("core",))
    placed = (split, P("atoms", None), split, P(), P())
    return jax.shard_map(
        shards, mesh=fine, in_specs=placed, out_specs=P("atoms", None), check_vma=False
    )
```

```python
import jax
import jax.numpy as jnp
from jax import lax
from jax.experimental import pallas as pl
from jax.experimental.pallas import tpu as pltpu
from jax.sharding import Mesh, PartitionSpec as P

NB = 24
BLOCK = NB * NB
SLOTS = 2
ROWS, ACROSS, CORES = 2, 4, 2
COLUMNS = ROWS * ACROSS
LANES = 128
COLUMN_AXES = ("row", "across")
CHIP_AXES = ("line",) + COLUMN_AXES
BF16 = jnp.bfloat16
F32 = jnp.float32
SMALL = pltpu.CompilerParams(vmem_limit_bytes=4 * 2**20)
LARGE = pltpu.CompilerParams(vmem_limit_bytes=16 * 2**20)


def split_two(x):
    high = x.astype(BF16)
    return high, (x - high.astype(F32)).astype(BF16)


def match(shape, dim_a, div_a, dim_b, div_b, mod_a=None, mod_b=None):
    a = lax.broadcasted_iota(jnp.int32, shape, dim_a) // div_a
    b = lax.broadcasted_iota(jnp.int32, shape, dim_b) // div_b
    a = a if mod_a is None else a % mod_a
    b = b if mod_b is None else b % mod_b
    return a == b


def dot(a, b):
    return jnp.dot(a, b, preferred_element_type=F32)


def iota(shape, dim):
    return lax.broadcasted_iota(jnp.int32, shape, dim)


def one_hot(condition):
    return condition.astype(F32).astype(BF16)


def leaving_kernel(atoms_hbm, home_hbm, metric_hbm, rows_hbm, leaving_ref, pick_ref, terms_ref, atoms_ref, home_ref, metric_ref, rows_ref, sems):
    fetches = [
        pltpu.make_async_copy(source, target, sems.at[i])
        for i, (source, target) in enumerate(
            [(atoms_hbm, atoms_ref), (home_hbm, home_ref), (metric_hbm, metric_ref), (rows_hbm, rows_ref)]
        )
    ]
    for fetch in fetches:
        fetch.start()
    me = lax.axis_index("atoms")
    groups = leaving_ref.shape[0]
    stored = rows_ref.shape[0]
    chunks, lanes = home_ref.shape
    total = atoms_ref.shape[1]
    pairs = total // groups
    fetches[0].wait()
    fetches[1].wait()
    home = home_ref[...]
    owner_of = lax.div(home, stored).astype(F32).astype(BF16)
    within_of = lax.rem(home, stored).astype(F32).astype(BF16)
    square = (total, total)
    same = iota(square, 0) == iota(square, 1)
    before = iota(square, 0) < iota(square, 1)

    def column(x):
        return jnp.sum(jnp.where(same, x, 0.0), axis=1, keepdims=True)

    def count(condition):
        return jnp.sum(jnp.where(condition, 1.0, 0.0), axis=0, keepdims=True)

    group_row = lax.div(iota((1, total), 1), pairs).astype(F32)
    owner, within, key_row, key_column = [], [], [], []
    for side in range(2):
        atom = atoms_ref[side : side + 1, :]
        hit = one_hot(iota((lanes, total), 0) == lax.rem(atom, lanes))
        chunk = iota((chunks, total), 0) == lax.div(atom, lanes)
        owner.append(jnp.sum(jnp.where(chunk, dot(owner_of, hit), 0.0), axis=0, keepdims=True))
        within.append(jnp.sum(jnp.where(chunk, dot(within_of, hit), 0.0), axis=0, keepdims=True))
        key_row.append(group_row * groups + owner[side])
        key_column.append(column(key_row[side]))
    slot = [
        count((key_column[0] == key_row[0]) & before),
        count(key_column[0] == key_row[1]) + count((key_column[1] == key_row[1]) & before),
    ]
    sends = groups * SLOTS
    spots = (sends, total)
    dest = lax.div(iota(spots, 1), pairs) == lax.div(iota(spots, 0), SLOTS)
    turn = lax.rem(iota(spots, 0), SLOTS).astype(F32)
    entries = (2 * pairs, total)
    mine = iota(entries, 1) == me * pairs + lax.div(iota(entries, 0), 2)
    out, pick = 0.0, 0.0
    for side in range(2):
        chosen = dest & (slot[side] == turn) & (owner[side] == me.astype(F32))
        stored_at = column(within[side]).astype(jnp.int32) == iota((total, stored), 1)
        out += dot(one_hot(chosen), one_hot(stored_at))
        place = column(owner[side] * SLOTS + slot[side]).astype(jnp.int32)
        arrives = place == iota((total, sends), 1)
        local = mine & (lax.rem(iota(entries, 0), 2) == side)
        pick += dot(one_hot(local), one_hot(arrives))
    pick_ref[...] = pick.astype(BF16)
    fetches[2].wait()
    local_aux, all_aux = metric_ref.shape[1:]
    square = (all_aux, all_aux)
    chips = all_aux // (CORES * local_aux)
    core = lax.rem(lax.div(iota(square, 0), local_aux), CORES)
    target = lax.rem(iota(square, 0), local_aux) * CORES + core
    target = target * chips + lax.div(iota(square, 0), CORES * local_aux)
    order = one_hot(target == iota(square, 1))
    twice = (2 * pairs, pairs)
    owns = lax.div(iota(twice, 0), 2) == iota(twice, 1)
    term = lax.rem(iota(twice, 0), 2)
    for q in range(local_aux):
        high, low = split_two(metric_ref[:, q, :])
        both = dot(one_hot(owns & (term == 0)), high) + dot(one_hot(owns & (term == 1)), low)
        both = dot(both.astype(BF16), order).astype(BF16)
        terms_ref[:, q * all_aux : (q + 1) * all_aux] = both
    fetches[3].wait()
    leaving = dot(out.astype(BF16), rows_ref[...]).astype(BF16)
    leaving_ref[...] = leaving.reshape(leaving_ref.shape)


def message_kernel(arrived_ref, pick_ref, metric_ref, density_ref, message_ref, block_ref):
    pairs = metric_ref.shape[0] // 2
    chips = message_ref.shape[0]
    arrived = arrived_ref[...].reshape(pick_ref.shape[1], arrived_ref.shape[2])
    rows = dot(pick_ref[...], arrived).astype(BF16)
    rows = jnp.concatenate([rows, metric_ref[...]], axis=1).reshape(pairs, 2, -1)
    empty = jnp.zeros((COLUMNS - pairs,) + rows.shape[1:], BF16)
    for line in range(0, chips, COLUMNS):
        message_ref[line : line + pairs] = rows
        message_ref[line + pairs : line + COLUMNS] = empty
    mine = lax.axis_index("row") * ACROSS + lax.axis_index("across")
    mine = iota((pairs, 1), 0) == jnp.minimum(mine, pairs - 1)
    block = jnp.sum(jnp.where(mine, density_ref[...].astype(F32), 0.0), axis=0, keepdims=True)
    block = jnp.where(match((NB, BLOCK), 0, 1, 1, NB), block, 0.0).astype(BF16)
    block_ref[...] = dot(block, match((BLOCK, NB), 0, 1, 1, 1, mod_a=NB).astype(BF16)).astype(BF16)


def exchange_kernel(own_ref, second_ref, block_ref, out_ref):
    count = own_ref.shape[0]
    half, width = count // 2, second_ref.shape[1]
    row = lax.broadcasted_iota(jnp.int32, (count, count), 0)
    column = lax.broadcasted_iota(jnp.int32, (count, count), 1)
    picked = jnp.where(row < half, 2 * row, 2 * (row - half) + 1) == column
    own = dot(picked.astype(BF16), own_ref[...]).astype(BF16)
    first = own[:half, :width]
    first = jnp.concatenate([first[:, :BLOCK], first[:, BLOCK:]], 0)
    terms = own[:, width:]
    aux = terms.shape[1] // 2
    high = jnp.concatenate([terms[:half, :aux], terms[:half, aux:]], 0)
    low = jnp.concatenate([terms[half:, :aux], terms[half:, aux:]], 0)
    second = second_ref[...]
    second = jnp.concatenate([second[:, :BLOCK], second[:, BLOCK:]], 0)
    mixed = dot(high, second) + dot(low, second)
    high, low = split_two(mixed)
    gram = lax.dot_general(
        jnp.concatenate([first, first], 0),
        jnp.concatenate([high, low], 0),
        (((0,), (0,)), ((), ())),
        preferred_element_type=F32,
    )
    spread = match((NB, BLOCK), 0, 1, 1, 1, mod_b=NB).astype(BF16)
    weight = dot(block_ref[...], spread)
    top = jnp.sum(gram.reshape(NB, NB, BLOCK) * weight[None], axis=1)
    high, low = split_two(top)
    fold = match((BLOCK, BLOCK), 0, NB, 1, 1, mod_b=NB).astype(BF16)
    flat = dot(high, fold) + dot(low, fold)
    keep = match((NB, BLOCK), 0, 1, 1, NB)
    flat = jnp.sum(jnp.where(keep, flat, 0.0), axis=0, keepdims=True)
    out_ref[...] = jnp.broadcast_to(flat[None], out_ref.shape)


def shards(coefficients, density, metric, pair_atoms, home_row):
    groups = lax.axis_size("atoms")
    columns = lax.axis_size(COLUMN_AXES)
    chips = lax.axis_size(CHIP_AXES)
    cores = lax.axis_size("core")
    width = coefficients.shape[1]
    pairs = density.shape[0]
    entries = 2 * pairs
    local_aux = width // BLOCK
    all_aux = chips * cores * local_aux

    in_hbm = pl.BlockSpec(memory_space=pltpu.HBM)
    in_vmem = pl.BlockSpec(memory_space=pltpu.VMEM)
    sources = [pair_atoms.T, home_row.reshape(-1, LANES), metric, coefficients]
    leaving, pick, terms = pl.pallas_call(
        leaving_kernel,
        in_specs=[in_hbm] * 4,
        out_specs=[in_vmem] * 3,
        out_shape=[
            jax.ShapeDtypeStruct((groups, SLOTS, width), BF16),
            jax.ShapeDtypeStruct((entries, groups * SLOTS), BF16),
            jax.ShapeDtypeStruct((entries, local_aux * all_aux), BF16),
        ],
        scratch_shapes=[pltpu.VMEM(x.shape, x.dtype) for x in sources] + [pltpu.SemaphoreType.DMA((4,))],
    )(*sources)
    arrived = lax.all_to_all(leaving, "atoms", 0, 0)

    message, block = pl.pallas_call(
        message_kernel,
        in_specs=[in_vmem] * 4,
        out_specs=[in_vmem] * 2,
        out_shape=[
            jax.ShapeDtypeStruct((chips, 2, width + local_aux * all_aux), BF16),
            jax.ShapeDtypeStruct((NB, NB), BF16),
        ],
        compiler_params=SMALL,
    )(arrived, pick, terms, density)
    everyone = lax.all_to_all(message, CHIP_AXES, 0, 0)

    second = lax.all_gather(everyone[:, 1, :width], "core", axis=0, tiled=True)
    out = pl.pallas_call(
        exchange_kernel,
        out_shape=jax.ShapeDtypeStruct((columns * cores, 1, BLOCK), F32),
        compiler_params=LARGE,
    )(everyone.reshape(chips * 2, -1), second, block)
    parts = lax.all_to_all(out, COLUMN_AXES + ("core",), 0, 0)
    return jnp.sum(parts.reshape(columns, cores, BLOCK), axis=1)[:pairs]


def solution(mesh):
    atoms, aux = mesh.devices.shape
    fine = mesh.devices.reshape(atoms, aux // (ROWS * ACROSS * CORES), ROWS, ACROSS, CORES)
    fine = Mesh(fine, ("atoms", "line", "row", "across", "core"))
    split = P("atoms", CHIP_AXES + ("core",))
    placed = (split, P("atoms", None), split, P(), P())
    return jax.shard_map(
        shards, mesh=fine, in_specs=placed, out_specs=P("atoms", None), check_vma=False
    )
```

```python
import jax
import jax.numpy as jnp
from jax import lax
from jax.experimental import pallas as pl
from jax.experimental.pallas import tpu as pltpu
from jax.sharding import Mesh, PartitionSpec as P

NB = 24
BLOCK = NB * NB
SLOTS = 2
ROWS, ACROSS, CORES = 2, 4, 2
COLUMNS = ROWS * ACROSS
LANES = 128
LOCAL_AUX = 2
STEP = 4
FLOPS, BYTES = 10**9, 10**6
COLUMN_AXES = ("row", "across")
CHIP_AXES = ("line",) + COLUMN_AXES
BF16 = jnp.bfloat16
F32 = jnp.float32
SMALL = pltpu.CompilerParams(vmem_limit_bytes=4 * 2**20)
LARGE = pltpu.CompilerParams(vmem_limit_bytes=16 * 2**20)


def split_two(x):
    high = x.astype(BF16)
    return high, (x - high.astype(F32)).astype(BF16)


def dot(a, b):
    return jnp.dot(a, b, preferred_element_type=F32)


def dot_lanes(a, b):
    return lax.dot_general(a, b, (((1,), (1,)), ((), ())), preferred_element_type=F32)


def iota(shape, dim):
    return lax.broadcasted_iota(jnp.int32, shape, dim)


def one_hot(condition):
    return condition.astype(F32).astype(BF16)


def layout_kernel(layout_ref, order_ref):
    place = iota((1, BLOCK), 1)
    major = lax.div(place, NB)
    index = iota((NB, BLOCK), 0)
    layout_ref[0] = one_hot(index == major)
    layout_ref[1] = one_hot(index == place - major * NB)
    square = order_ref.shape
    chips = square[0] // (CORES * LOCAL_AUX)
    function = iota((square[0], 1), 0)
    core = lax.rem(lax.div(function, LOCAL_AUX), CORES)
    target = lax.rem(function, LOCAL_AUX) * CORES + core
    target = target * chips + lax.div(function, CORES * LOCAL_AUX)
    order_ref[...] = one_hot(target == iota(square, 1))


def leaving_kernel(atoms_ref, home_ref, metric_ref, order_ref, rows_ref, leaving_ref, pick_ref, terms_ref):
    me = lax.axis_index("atoms")
    groups = leaving_ref.shape[0]
    stored = rows_ref.shape[0]
    chunks, lanes = home_ref.shape
    total = atoms_ref.shape[1]
    pairs = total // groups
    home = home_ref[...]
    owner_of = lax.div(home, stored).astype(F32).astype(BF16)
    within_of = lax.rem(home, stored).astype(F32).astype(BF16)
    square = (total, total)
    same = iota(square, 0) == iota(square, 1)
    before = iota(square, 0) < iota(square, 1)

    def column(x):
        return jnp.sum(jnp.where(same, x, 0.0), axis=1, keepdims=True)

    def count(condition):
        return jnp.sum(jnp.where(condition, 1.0, 0.0), axis=0, keepdims=True)

    group_row = lax.div(iota((1, total), 1), pairs).astype(F32)
    owner, within, key_row, key_column = [], [], [], []
    for side in range(2):
        atom = atoms_ref[side : side + 1, :]
        hit = one_hot(iota((lanes, total), 0) == lax.rem(atom, lanes))
        chunk = iota((chunks, total), 0) == lax.div(atom, lanes)
        owner.append(jnp.sum(jnp.where(chunk, dot(owner_of, hit), 0.0), axis=0, keepdims=True))
        within.append(jnp.sum(jnp.where(chunk, dot(within_of, hit), 0.0), axis=0, keepdims=True))
        key_row.append(group_row * groups + owner[side])
        key_column.append(column(key_row[side]))
    slot = [
        count((key_column[0] == key_row[0]) & before),
        count(key_column[0] == key_row[1]) + count((key_column[1] == key_row[1]) & before),
    ]
    sends = groups * SLOTS
    spots = (sends, total)
    dest = lax.div(iota(spots, 1), pairs) == lax.div(iota(spots, 0), SLOTS)
    turn = lax.rem(iota(spots, 0), SLOTS).astype(F32)
    entries = (2 * pairs, total)
    mine = iota(entries, 1) == me * pairs + lax.div(iota(entries, 0), 2)
    out, pick = 0.0, 0.0
    for side in range(2):
        chosen = dest & (slot[side] == turn) & (owner[side] == me.astype(F32))
        stored_at = column(within[side]).astype(jnp.int32) == iota((total, stored), 1)
        out += dot(one_hot(chosen), one_hot(stored_at))
        place = column(owner[side] * SLOTS + slot[side]).astype(jnp.int32)
        arrives = place == iota((total, sends), 1)
        local = mine & (lax.rem(iota(entries, 0), 2) == side)
        pick += dot(one_hot(local), one_hot(arrives))
    pick_ref[...] = pick.astype(BF16)
    local_aux, all_aux = metric_ref.shape[1:]
    twice = (2 * pairs, pairs)
    owns = lax.div(iota(twice, 0), 2) == iota(twice, 1)
    term = lax.rem(iota(twice, 0), 2)
    for q in range(local_aux):
        high, low = split_two(metric_ref[:, q, :])
        both = dot(one_hot(owns & (term == 0)), high) + dot(one_hot(owns & (term == 1)), low)
        both = dot(both.astype(BF16), order_ref[...]).astype(BF16)
        terms_ref[:, q * all_aux : (q + 1) * all_aux] = both
    leaving = dot(out.astype(BF16), rows_ref[...]).astype(BF16)
    leaving_ref[...] = leaving.reshape(leaving_ref.shape)


def message_kernel(arrived_ref, pick_ref, metric_ref, density_ref, layout_ref, message_ref, block_ref):
    pairs = metric_ref.shape[0] // 2
    chips = message_ref.shape[0]
    arrived = arrived_ref[...].reshape(pick_ref.shape[1], arrived_ref.shape[2])
    rows = dot(pick_ref[...], arrived).astype(BF16)
    rows = jnp.concatenate([rows, metric_ref[...]], axis=1).reshape(pairs, 2, -1)
    empty = jnp.zeros((COLUMNS - pairs,) + rows.shape[1:], BF16)
    for line in range(0, chips, COLUMNS):
        message_ref[line : line + pairs] = rows
        message_ref[line + pairs : line + COLUMNS] = empty
    mine = lax.axis_index("row") * ACROSS + lax.axis_index("across")
    mine = iota((pairs, 1), 0) == jnp.minimum(mine, pairs - 1)
    block = jnp.sum(jnp.where(mine, density_ref[...].astype(F32), 0.0), axis=0, keepdims=True)
    segment, spread = layout_ref[0], layout_ref[1]
    block_ref[...] = dot_lanes((block * segment.astype(F32)).astype(BF16), spread).astype(BF16)


def exchange_kernel(own_ref, second_ref, block_ref, layout_ref, out_ref):
    count = own_ref.shape[0]
    half, width = count // 2, second_ref.shape[1]
    row = lax.broadcasted_iota(jnp.int32, (count, count), 0)
    column = lax.broadcasted_iota(jnp.int32, (count, count), 1)
    picked = jnp.where(row < half, 2 * row, 2 * (row - half) + 1) == column
    own = dot(picked.astype(BF16), own_ref[...]).astype(BF16)
    first = own[:half, :width]
    first = jnp.concatenate([first[:, :BLOCK], first[:, BLOCK:]], 0)
    terms = own[:, width:]
    aux = terms.shape[1] // 2
    high = jnp.concatenate([terms[:half, :aux], terms[:half, aux:]], 0)
    low = jnp.concatenate([terms[half:, :aux], terms[half:, aux:]], 0)
    second = second_ref[...]
    second = jnp.concatenate([second[:, :BLOCK], second[:, BLOCK:]], 0)
    mixed = dot(high, second) + dot(low, second)
    high, low = split_two(mixed)
    first = jnp.concatenate([first, first], 0).T
    mixed = jnp.concatenate([high, low], 0)
    segment, spread = layout_ref[0], layout_ref[1]
    weight = dot(block_ref[...], spread)[None]
    tops = []
    for m in range(0, NB, STEP):
        gram = dot(first[m * NB : (m + STEP) * NB], mixed)
        tops.append(jnp.sum(gram.reshape(STEP, NB, BLOCK) * weight, axis=1))
    top = jnp.concatenate(tops, 0)
    high, low = split_two(top)
    high, low = split_two(dot_lanes(high, segment) + dot_lanes(low, segment))
    flat = (dot(high, spread) + dot(low, spread)) * segment.astype(F32)
    flat = jnp.sum(flat, axis=0, keepdims=True)
    out_ref[...] = jnp.broadcast_to(flat[None], out_ref.shape)


def shards(coefficients, density, metric, pair_atoms, home_row):
    groups = lax.axis_size("atoms")
    columns = lax.axis_size(COLUMN_AXES)
    chips = lax.axis_size(CHIP_AXES)
    cores = lax.axis_size("core")
    width = coefficients.shape[1]
    pairs = density.shape[0]
    entries = 2 * pairs
    local_aux = width // BLOCK
    all_aux = chips * cores * local_aux

    in_vmem = pl.BlockSpec(memory_space=pltpu.VMEM)
    layout, order = pl.pallas_call(
        layout_kernel,
        out_specs=[in_vmem] * 2,
        out_shape=[
            jax.ShapeDtypeStruct((2, NB, BLOCK), BF16),
            jax.ShapeDtypeStruct((all_aux, all_aux), BF16),
        ],
        compiler_params=SMALL,
        cost_estimate=pl.CostEstimate(flops=FLOPS, bytes_accessed=BYTES, transcendentals=0),
    )()
    sources = [pair_atoms.T, home_row.reshape(-1, LANES), metric, order, coefficients]
    leaving, pick, terms = pl.pallas_call(
        leaving_kernel,
        in_specs=[in_vmem] * 5,
        out_specs=[in_vmem] * 3,
        out_shape=[
            jax.ShapeDtypeStruct((groups, SLOTS, width), BF16),
            jax.ShapeDtypeStruct((entries, groups * SLOTS), BF16),
            jax.ShapeDtypeStruct((entries, local_aux * all_aux), BF16),
        ],
        compiler_params=SMALL,
    )(*sources)
    arrived = lax.all_to_all(leaving, "atoms", 0, 0)

    message, block = pl.pallas_call(
        message_kernel,
        in_specs=[in_vmem] * 5,
        out_specs=[in_vmem] * 2,
        out_shape=[
            jax.ShapeDtypeStruct((chips, 2, width + local_aux * all_aux), BF16),
            jax.ShapeDtypeStruct((NB, NB), BF16),
        ],
        compiler_params=SMALL,
    )(arrived, pick, terms, density, layout)
    everyone = lax.all_to_all(message, CHIP_AXES, 0, 0)

    second = lax.all_gather(everyone[:, 1, :width], "core", axis=0, tiled=True)
    out = pl.pallas_call(
        exchange_kernel,
        out_shape=jax.ShapeDtypeStruct((columns * cores, 1, BLOCK), F32),
        compiler_params=LARGE,
    )(everyone.reshape(chips * 2, -1), second, block, layout)
    parts = lax.all_to_all(out, COLUMN_AXES + ("core",), 0, 0)
    return jnp.sum(parts.reshape(columns, cores, BLOCK), axis=1)[:pairs]


def solution(mesh):
    atoms, aux = mesh.devices.shape
    fine = mesh.devices.reshape(atoms, aux // (ROWS * ACROSS * CORES), ROWS, ACROSS, CORES)
    fine = Mesh(fine, ("atoms", "line", "row", "across", "core"))
    split = P("atoms", CHIP_AXES + ("core",))
    placed = (split, P("atoms", None), split, P(), P())
    return jax.shard_map(
        shards, mesh=fine, in_specs=placed, out_specs=P("atoms", None), check_vma=False
    )
```

```python
import jax
import jax.numpy as jnp
from jax import lax
from jax.experimental import pallas as pl
from jax.experimental.pallas import tpu as pltpu
from jax.sharding import Mesh, PartitionSpec as P

NB = 24
BLOCK = NB * NB
SLOTS = 2
ROWS, ACROSS, CORES = 2, 4, 2
COLUMNS = ROWS * ACROSS
LANES = 128
LOCAL_AUX = 2
STEP = 4
FLOPS, BYTES = 10**9, 10**6
COLUMN_AXES = ("row", "across")
CHIP_AXES = ("line",) + COLUMN_AXES
BF16 = jnp.bfloat16
F32 = jnp.float32
SMALL = pltpu.CompilerParams(vmem_limit_bytes=4 * 2**20)
LARGE = pltpu.CompilerParams(vmem_limit_bytes=16 * 2**20)


def split_two(x):
    high = x.astype(BF16)
    return high, (x - high.astype(F32)).astype(BF16)


def dot(a, b):
    return jnp.dot(a, b, preferred_element_type=F32)


def dot_lanes(a, b):
    return lax.dot_general(a, b, (((1,), (1,)), ((), ())), preferred_element_type=F32)


def iota(shape, dim):
    return lax.broadcasted_iota(jnp.int32, shape, dim)


def one_hot(condition):
    return condition.astype(F32).astype(BF16)


def layout_kernel(layout_ref, order_ref):
    place = iota((1, BLOCK), 1)
    major = lax.div(place, NB)
    index = iota((NB, BLOCK), 0)
    layout_ref[0] = one_hot(index == major)
    layout_ref[1] = one_hot(index == place - major * NB)
    square = order_ref.shape
    chips = square[0] // (CORES * LOCAL_AUX)
    function = iota((square[0], 1), 0)
    core = lax.rem(lax.div(function, LOCAL_AUX), CORES)
    target = lax.rem(function, LOCAL_AUX) * CORES + core
    target = target * chips + lax.div(function, CORES * LOCAL_AUX)
    order_ref[...] = one_hot(target == iota(square, 1))


def leaving_kernel(atoms_ref, home_ref, metric_ref, order_ref, rows_ref, leaving_ref, pick_ref, terms_ref):
    me = lax.axis_index("atoms")
    groups = leaving_ref.shape[0]
    stored = rows_ref.shape[0]
    chunks, lanes = home_ref.shape
    total = atoms_ref.shape[1]
    pairs = total // groups
    home = home_ref[...]
    owner_of = lax.div(home, stored).astype(F32).astype(BF16)
    within_of = lax.rem(home, stored).astype(F32).astype(BF16)
    square = (total, total)
    same = iota(square, 0) == iota(square, 1)
    before = iota(square, 0) < iota(square, 1)

    def column(x):
        return jnp.sum(jnp.where(same, x, 0.0), axis=1, keepdims=True)

    def count(condition):
        return jnp.sum(jnp.where(condition, 1.0, 0.0), axis=0, keepdims=True)

    group_row = lax.div(iota((1, total), 1), pairs).astype(F32)
    owner, within, key_row, key_column = [], [], [], []
    for side in range(2):
        atom = atoms_ref[side : side + 1, :]
        hit = one_hot(iota((lanes, total), 0) == lax.rem(atom, lanes))
        chunk = iota((chunks, total), 0) == lax.div(atom, lanes)
        owner.append(jnp.sum(jnp.where(chunk, dot(owner_of, hit), 0.0), axis=0, keepdims=True))
        within.append(jnp.sum(jnp.where(chunk, dot(within_of, hit), 0.0), axis=0, keepdims=True))
        key_row.append(group_row * groups + owner[side])
        key_column.append(column(key_row[side]))
    slot = [
        count((key_column[0] == key_row[0]) & before),
        count(key_column[0] == key_row[1]) + count((key_column[1] == key_row[1]) & before),
    ]
    sends = groups * SLOTS
    spots = (sends, total)
    dest = lax.div(iota(spots, 1), pairs) == lax.div(iota(spots, 0), SLOTS)
    turn = lax.rem(iota(spots, 0), SLOTS).astype(F32)
    entries = (2 * pairs, total)
    mine = iota(entries, 1) == me * pairs + lax.div(iota(entries, 0), 2)
    out, pick = 0.0, 0.0
    for side in range(2):
        chosen = dest & (slot[side] == turn) & (owner[side] == me.astype(F32))
        stored_at = column(within[side]).astype(jnp.int32) == iota((total, stored), 1)
        out += dot(one_hot(chosen), one_hot(stored_at))
        place = column(owner[side] * SLOTS + slot[side]).astype(jnp.int32)
        arrives = place == iota((total, sends), 1)
        local = mine & (lax.rem(iota(entries, 0), 2) == side)
        pick += dot(one_hot(local), one_hot(arrives))
    pick_ref[...] = pick.astype(BF16)
    local_aux, all_aux = metric_ref.shape[1:]
    twice = (2 * pairs, pairs)
    owns = lax.div(iota(twice, 0), 2) == iota(twice, 1)
    term = lax.rem(iota(twice, 0), 2)
    for q in range(local_aux):
        high, low = split_two(metric_ref[:, q, :])
        both = dot(one_hot(owns & (term == 0)), high) + dot(one_hot(owns & (term == 1)), low)
        both = dot(both.astype(BF16), order_ref[...]).astype(BF16)
        terms_ref[:, q * all_aux : (q + 1) * all_aux] = both
    leaving = dot(out.astype(BF16), rows_ref[...]).astype(BF16)
    leaving_ref[...] = leaving.reshape(leaving_ref.shape)


def message_kernel(arrived_ref, pick_ref, metric_ref, density_ref, layout_ref, message_ref, block_ref):
    pairs = metric_ref.shape[0] // 2
    chips = message_ref.shape[0]
    arrived = arrived_ref[...].reshape(pick_ref.shape[1], arrived_ref.shape[2])
    rows = dot(pick_ref[...], arrived).astype(BF16)
    rows = jnp.concatenate([rows, metric_ref[...]], axis=1).reshape(pairs, 2, -1)
    empty = jnp.zeros((COLUMNS - pairs,) + rows.shape[1:], BF16)
    for line in range(0, chips, COLUMNS):
        message_ref[line : line + pairs] = rows
        message_ref[line + pairs : line + COLUMNS] = empty
    mine = lax.axis_index("row") * ACROSS + lax.axis_index("across")
    mine = iota((pairs, 1), 0) == jnp.minimum(mine, pairs - 1)
    block = jnp.sum(jnp.where(mine, density_ref[...].astype(F32), 0.0), axis=0, keepdims=True)
    segment, spread = layout_ref[0], layout_ref[1]
    block_ref[...] = dot_lanes((block * segment.astype(F32)).astype(BF16), spread).astype(BF16)


def exchange_kernel(given_ref, block_ref, layout_ref, out_ref):
    count = given_ref.shape[0]
    half = count // 2
    row, column = iota((count, count), 0), iota((count, count), 1)
    picked = jnp.where(row < half, 2 * row, 2 * (row - half) + 1) == column
    given = dot(picked.astype(BF16), given_ref[...]).astype(BF16)

    def stacked(part, start, width):
        part = part[:, start : start + LOCAL_AUX * width]
        return jnp.concatenate([part[:, q * width : (q + 1) * width] for q in range(LOCAL_AUX)], 0)

    first, second = stacked(given[:half], 0, BLOCK), stacked(given[half:], 0, BLOCK)
    terms = LOCAL_AUX * BLOCK
    high, low = stacked(given[:half], terms, count), stacked(given[half:], terms, count)
    mixed = dot(high, second) + dot(low, second)
    high, low = split_two(mixed)
    first = jnp.concatenate([first, first], 0).T
    mixed = jnp.concatenate([high, low], 0)
    segment, spread = layout_ref[0], layout_ref[1]
    weight = dot(block_ref[...], spread)[None]
    tops = []
    for m in range(0, NB, STEP):
        gram = dot(first[m * NB : (m + STEP) * NB], mixed)
        tops.append(jnp.sum(gram.reshape(STEP, NB, BLOCK) * weight, axis=1))
    top = jnp.concatenate(tops, 0)
    high, low = split_two(top)
    high, low = split_two(dot_lanes(high, segment) + dot_lanes(low, segment))
    flat = (dot(high, spread) + dot(low, spread)) * segment.astype(F32)
    flat = jnp.sum(flat, axis=0, keepdims=True)
    out_ref[...] = jnp.broadcast_to(flat[None], out_ref.shape)


def shards(coefficients, density, metric, pair_atoms, home_row):
    groups = lax.axis_size("atoms")
    columns = lax.axis_size(COLUMN_AXES)
    chips = lax.axis_size(CHIP_AXES)
    cores = lax.axis_size("core")
    width = coefficients.shape[1]
    pairs = density.shape[0]
    entries = 2 * pairs
    local_aux = width // BLOCK
    all_aux = chips * cores * local_aux

    in_vmem = pl.BlockSpec(memory_space=pltpu.VMEM)
    layout, order = pl.pallas_call(
        layout_kernel,
        out_specs=[in_vmem] * 2,
        out_shape=[
            jax.ShapeDtypeStruct((2, NB, BLOCK), BF16),
            jax.ShapeDtypeStruct((all_aux, all_aux), BF16),
        ],
        compiler_params=SMALL,
        cost_estimate=pl.CostEstimate(flops=FLOPS, bytes_accessed=BYTES, transcendentals=0),
    )()
    sources = [pair_atoms.T, home_row.reshape(-1, LANES), metric, order, coefficients]
    leaving, pick, terms = pl.pallas_call(
        leaving_kernel,
        in_specs=[in_vmem] * 5,
        out_specs=[in_vmem] * 3,
        out_shape=[
            jax.ShapeDtypeStruct((groups, SLOTS, width), BF16),
            jax.ShapeDtypeStruct((entries, groups * SLOTS), BF16),
            jax.ShapeDtypeStruct((entries, local_aux * all_aux), BF16),
        ],
        compiler_params=SMALL,
    )(*sources)
    arrived = lax.all_to_all(leaving, "atoms", 0, 0)

    message, block = pl.pallas_call(
        message_kernel,
        in_specs=[in_vmem] * 5,
        out_specs=[in_vmem] * 2,
        out_shape=[
            jax.ShapeDtypeStruct((chips, 2, width + local_aux * all_aux), BF16),
            jax.ShapeDtypeStruct((NB, NB), BF16),
        ],
        compiler_params=SMALL,
    )(arrived, pick, terms, density, layout)
    everyone = lax.all_to_all(message, CHIP_AXES, 0, 0)

    given = lax.all_gather(everyone, "core", axis=0, tiled=True)
    out = pl.pallas_call(
        exchange_kernel,
        out_shape=jax.ShapeDtypeStruct((columns, 1, BLOCK), F32),
        compiler_params=LARGE,
    )(given.reshape(chips * cores * 2, -1), block, layout)
    return lax.all_to_all(out, COLUMN_AXES, 0, 0)[:pairs, 0]


def solution(mesh):
    atoms, aux = mesh.devices.shape
    fine = mesh.devices.reshape(atoms, aux // (ROWS * ACROSS * CORES), ROWS, ACROSS, CORES)
    fine = Mesh(fine, ("atoms", "line", "row", "across", "core"))
    split = P("atoms", CHIP_AXES + ("core",))
    placed = (split, P("atoms", None), split, P(), P())
    return jax.shard_map(
        shards, mesh=fine, in_specs=placed, out_specs=P("atoms", None), check_vma=False
    )
```

```python
import jax
import jax.numpy as jnp
from jax import lax
from jax.experimental import pallas as pl
from jax.experimental.pallas import tpu as pltpu
from jax.sharding import Mesh, PartitionSpec as P

NB = 24
BLOCK = NB * NB
SLOTS = 2
ROWS, ACROSS, CORES = 2, 4, 2
COLUMNS = ROWS * ACROSS
LANES = 128
LOCAL_AUX = 2
STEP = 8
SHRINK, FLOOR = 2.0**-10, 1e-30
FLOPS, BYTES = 10**9, 10**6
COLUMN_AXES = ("row", "across")
CHIP_AXES = ("line",) + COLUMN_AXES
BF16 = jnp.bfloat16
F32 = jnp.float32
SMALL = pltpu.CompilerParams(vmem_limit_bytes=4 * 2**20)
LARGE = pltpu.CompilerParams(vmem_limit_bytes=16 * 2**20)


def split_two(x):
    high = x.astype(BF16)
    return high, (x - high.astype(F32)).astype(BF16)


def dot(a, b):
    return jnp.dot(a, b, preferred_element_type=F32)


def dot_lanes(a, b):
    return lax.dot_general(a, b, (((1,), (1,)), ((), ())), preferred_element_type=F32)


def iota(shape, dim):
    return lax.broadcasted_iota(jnp.int32, shape, dim)


def one_hot(condition):
    return condition.astype(F32).astype(BF16)


def layout_kernel(layout_ref, order_ref):
    place = iota((1, BLOCK), 1)
    major = lax.div(place, NB)
    index = iota((NB, BLOCK), 0)
    layout_ref[0] = one_hot(index == major)
    layout_ref[1] = one_hot(index == place - major * NB)
    square = order_ref.shape
    chips = square[0] // (CORES * LOCAL_AUX)
    function = iota((square[0], 1), 0)
    core = lax.rem(lax.div(function, LOCAL_AUX), CORES)
    target = lax.rem(function, LOCAL_AUX) * CORES + core
    target = target * chips + lax.div(function, CORES * LOCAL_AUX)
    order_ref[...] = one_hot(target == iota(square, 1))


def leaving_kernel(atoms_ref, home_ref, metric_ref, order_ref, rows_ref, leaving_ref, pick_ref, terms_ref):
    me = lax.axis_index("atoms")
    groups = leaving_ref.shape[0]
    stored = rows_ref.shape[0]
    chunks, lanes = home_ref.shape
    total = atoms_ref.shape[1]
    pairs = total // groups
    home = home_ref[...]
    owner_of = lax.div(home, stored).astype(F32).astype(BF16)
    within_of = lax.rem(home, stored).astype(F32).astype(BF16)
    square = (total, total)
    same = iota(square, 0) == iota(square, 1)
    before = iota(square, 0) < iota(square, 1)

    def column(x):
        return jnp.sum(jnp.where(same, x, 0.0), axis=1, keepdims=True)

    def count(condition):
        return jnp.sum(jnp.where(condition, 1.0, 0.0), axis=0, keepdims=True)

    group_row = lax.div(iota((1, total), 1), pairs).astype(F32)
    owner, within, key_row, key_column = [], [], [], []
    for side in range(2):
        atom = atoms_ref[side : side + 1, :]
        hit = one_hot(iota((lanes, total), 0) == lax.rem(atom, lanes))
        chunk = iota((chunks, total), 0) == lax.div(atom, lanes)
        owner.append(jnp.sum(jnp.where(chunk, dot(owner_of, hit), 0.0), axis=0, keepdims=True))
        within.append(jnp.sum(jnp.where(chunk, dot(within_of, hit), 0.0), axis=0, keepdims=True))
        key_row.append(group_row * groups + owner[side])
        key_column.append(column(key_row[side]))
    slot = [
        count((key_column[0] == key_row[0]) & before),
        count(key_column[0] == key_row[1]) + count((key_column[1] == key_row[1]) & before),
    ]
    sends = groups * SLOTS
    spots = (sends, total)
    dest = lax.div(iota(spots, 1), pairs) == lax.div(iota(spots, 0), SLOTS)
    turn = lax.rem(iota(spots, 0), SLOTS).astype(F32)
    entries = (2 * pairs, total)
    mine = iota(entries, 1) == me * pairs + lax.div(iota(entries, 0), 2)
    out, pick = 0.0, 0.0
    for side in range(2):
        chosen = dest & (slot[side] == turn) & (owner[side] == me.astype(F32))
        stored_at = column(within[side]).astype(jnp.int32) == iota((total, stored), 1)
        out += dot(one_hot(chosen), one_hot(stored_at))
        place = column(owner[side] * SLOTS + slot[side]).astype(jnp.int32)
        arrives = place == iota((total, sends), 1)
        local = mine & (lax.rem(iota(entries, 0), 2) == side)
        pick += dot(one_hot(local), one_hot(arrives))
    pick_ref[...] = pick.astype(BF16)
    local_aux, all_aux = metric_ref.shape[1:]
    twice = (2 * pairs, pairs)
    owns = lax.div(iota(twice, 0), 2) == iota(twice, 1)
    term = lax.rem(iota(twice, 0), 2)
    for q in range(local_aux):
        high, low = split_two(metric_ref[:, q, :] * SHRINK)
        both = dot(one_hot(owns & (term == 0)), high) + dot(one_hot(owns & (term == 1)), low)
        both = dot(both.astype(BF16), order_ref[...]).astype(BF16)
        terms_ref[:, q * all_aux : (q + 1) * all_aux] = both
    leaving = dot(out.astype(BF16), rows_ref[...]).astype(BF16)
    leaving_ref[...] = leaving.reshape(leaving_ref.shape)


def message_kernel(arrived_ref, pick_ref, metric_ref, density_ref, layout_ref, message_ref, block_ref):
    pairs = metric_ref.shape[0] // 2
    chips = message_ref.shape[0]
    arrived = arrived_ref[...].reshape(pick_ref.shape[1], arrived_ref.shape[2])
    rows = dot(pick_ref[...], arrived).astype(BF16)
    rows = jnp.concatenate([rows, metric_ref[...]], axis=1).reshape(pairs, 2, -1)
    empty = jnp.zeros((COLUMNS - pairs,) + rows.shape[1:], BF16)
    for line in range(0, chips, COLUMNS):
        message_ref[line : line + pairs] = rows
        message_ref[line + pairs : line + COLUMNS] = empty
    mine = lax.axis_index("row") * ACROSS + lax.axis_index("across")
    mine = iota((pairs, 1), 0) == jnp.minimum(mine, pairs - 1)
    block = jnp.sum(jnp.where(mine, density_ref[...].astype(F32), 0.0), axis=0, keepdims=True)
    segment, spread = layout_ref[0], layout_ref[1]
    block_ref[...] = dot_lanes((block * segment.astype(F32)).astype(BF16), spread).astype(BF16)


def exchange_kernel(given_ref, block_ref, layout_ref, out_ref):
    count = given_ref.shape[0]
    half = count // 2
    row, column = iota((count, count), 0), iota((count, count), 1)
    picked = jnp.where(row < half, 2 * row, 2 * (row - half) + 1) == column
    given = dot(picked.astype(BF16), given_ref[...]).astype(BF16)

    def stacked(part, start, width):
        part = part[:, start : start + LOCAL_AUX * width]
        return jnp.concatenate([part[:, q * width : (q + 1) * width] for q in range(LOCAL_AUX)], 0)

    first, second = stacked(given[:half], 0, BLOCK), stacked(given[half:], 0, BLOCK)
    terms = LOCAL_AUX * BLOCK
    high, low = stacked(given[:half], terms, count), stacked(given[half:], terms, count)
    mixed = dot(high, second) + dot(low, second)
    largest = jnp.max(jnp.max(jnp.abs(mixed), axis=0, keepdims=True), axis=1, keepdims=True)
    largest = jnp.maximum(largest, FLOOR)
    high, low = split_two(mixed * (1.0 / largest))
    first = jnp.concatenate([first, first], 0).T
    mixed = jnp.concatenate([high, low], 0)
    segment, spread = layout_ref[0], layout_ref[1]
    weight = dot(block_ref[...], spread)[None]
    tops = []
    for m in range(0, NB, STEP):
        gram = dot(first[m * NB : (m + STEP) * NB], mixed)
        tops.append(jnp.sum(gram.reshape(STEP, NB, BLOCK) * weight, axis=1))
    top = jnp.concatenate(tops, 0)
    high, low = split_two(top)
    high, low = split_two(dot_lanes(high, segment) + dot_lanes(low, segment))
    flat = (dot(high, spread) + dot(low, spread)) * segment.astype(F32)
    flat = jnp.sum(flat, axis=0, keepdims=True) * largest * (1.0 / SHRINK)
    out_ref[...] = jnp.broadcast_to(flat[None], out_ref.shape)


def shards(coefficients, density, metric, pair_atoms, home_row):
    groups = lax.axis_size("atoms")
    columns = lax.axis_size(COLUMN_AXES)
    chips = lax.axis_size(CHIP_AXES)
    cores = lax.axis_size("core")
    width = coefficients.shape[1]
    pairs = density.shape[0]
    entries = 2 * pairs
    local_aux = width // BLOCK
    all_aux = chips * cores * local_aux

    in_vmem = pl.BlockSpec(memory_space=pltpu.VMEM)
    layout, order = pl.pallas_call(
        layout_kernel,
        out_specs=[in_vmem] * 2,
        out_shape=[
            jax.ShapeDtypeStruct((2, NB, BLOCK), BF16),
            jax.ShapeDtypeStruct((all_aux, all_aux), BF16),
        ],
        compiler_params=SMALL,
        cost_estimate=pl.CostEstimate(flops=FLOPS, bytes_accessed=BYTES, transcendentals=0),
    )()
    sources = [pair_atoms.T, home_row.reshape(-1, LANES), metric, order, coefficients]
    leaving, pick, terms = pl.pallas_call(
        leaving_kernel,
        in_specs=[in_vmem] * 5,
        out_specs=[in_vmem] * 3,
        out_shape=[
            jax.ShapeDtypeStruct((groups, SLOTS, width), BF16),
            jax.ShapeDtypeStruct((entries, groups * SLOTS), BF16),
            jax.ShapeDtypeStruct((entries, local_aux * all_aux), BF16),
        ],
        compiler_params=SMALL,
    )(*sources)
    arrived = lax.all_to_all(leaving, "atoms", 0, 0)

    message, block = pl.pallas_call(
        message_kernel,
        in_specs=[in_vmem] * 5,
        out_specs=[in_vmem] * 2,
        out_shape=[
            jax.ShapeDtypeStruct((chips, 2, width + local_aux * all_aux), BF16),
            jax.ShapeDtypeStruct((NB, NB), BF16),
        ],
        compiler_params=SMALL,
    )(arrived, pick, terms, density, layout)
    everyone = lax.all_to_all(message, CHIP_AXES, 0, 0)

    given = lax.all_gather(everyone, "core", axis=0, tiled=True)
    out = pl.pallas_call(
        exchange_kernel,
        out_shape=jax.ShapeDtypeStruct((columns, 1, BLOCK), F32),
        compiler_params=LARGE,
    )(given.reshape(chips * cores * 2, -1), block, layout)
    return lax.all_to_all(out, COLUMN_AXES, 0, 0)[:pairs, 0]


def solution(mesh):
    atoms, aux = mesh.devices.shape
    fine = mesh.devices.reshape(atoms, aux // (ROWS * ACROSS * CORES), ROWS, ACROSS, CORES)
    fine = Mesh(fine, ("atoms", "line", "row", "across", "core"))
    split = P("atoms", CHIP_AXES + ("core",))
    placed = (split, P("atoms", None), split, P(), P())
    return jax.shard_map(
        shards, mesh=fine, in_specs=placed, out_specs=P("atoms", None), check_vma=False
    )
```

```python
import jax
import jax.numpy as jnp
from jax import lax
from jax.experimental import pallas as pl
from jax.experimental.pallas import tpu as pltpu
from jax.sharding import Mesh, PartitionSpec as P

NB = 24
BLOCK = NB * NB
SLOTS = 2
ROWS, ACROSS, CORES = 2, 4, 2
COLUMNS = ROWS * ACROSS
LANES = 128
LOCAL_AUX = 2
STEP = 8
SHRINK, FLOOR = 2.0**-10, 1e-30
FLOPS, BYTES = 10**9, 10**6
COLUMN_AXES = ("row", "across")
CHIP_AXES = ("line",) + COLUMN_AXES
BF16 = jnp.bfloat16
F32 = jnp.float32
SMALL = pltpu.CompilerParams(vmem_limit_bytes=4 * 2**20)
LARGE = pltpu.CompilerParams(vmem_limit_bytes=16 * 2**20)


def split_two(x):
    high = x.astype(BF16)
    return high, (x - high.astype(F32)).astype(BF16)


def dot(a, b):
    return jnp.dot(a, b, preferred_element_type=F32)


def dot_lanes(a, b):
    return lax.dot_general(a, b, (((1,), (1,)), ((), ())), preferred_element_type=F32)


def iota(shape, dim):
    return lax.broadcasted_iota(jnp.int32, shape, dim)


def one_hot(condition):
    return condition.astype(F32).astype(BF16)


def layout_kernel(layout_ref, order_ref):
    place = iota((1, BLOCK), 1)
    major = lax.div(place, NB)
    index = iota((NB, BLOCK), 0)
    layout_ref[0] = one_hot(index == major)
    layout_ref[1] = one_hot(index == place - major * NB)
    square = order_ref.shape
    chips = square[0] // (CORES * LOCAL_AUX)
    function = iota((square[0], 1), 0)
    core = lax.rem(lax.div(function, LOCAL_AUX), CORES)
    target = lax.rem(function, LOCAL_AUX) * CORES + core
    target = target * chips + lax.div(function, CORES * LOCAL_AUX)
    order_ref[...] = one_hot(target == iota(square, 1))


def leaving_kernel(atoms_ref, home_ref, metric_ref, order_ref, rows_ref, leaving_ref, pick_ref, terms_ref):
    me = lax.axis_index("atoms")
    groups = leaving_ref.shape[0]
    stored = rows_ref.shape[0]
    chunks, lanes = home_ref.shape
    total = atoms_ref.shape[1]
    pairs = total // groups
    home = home_ref[...]
    owner_of = lax.div(home, stored).astype(F32).astype(BF16)
    within_of = lax.rem(home, stored).astype(F32).astype(BF16)
    square = (total, total)
    same = iota(square, 0) == iota(square, 1)
    before = iota(square, 0) < iota(square, 1)

    def column(x):
        return jnp.sum(jnp.where(same, x, 0.0), axis=1, keepdims=True)

    def count(condition):
        return jnp.sum(jnp.where(condition, 1.0, 0.0), axis=0, keepdims=True)

    group_row = lax.div(iota((1, total), 1), pairs).astype(F32)
    owner, within, key_row, key_column = [], [], [], []
    for side in range(2):
        atom = atoms_ref[side : side + 1, :]
        hit = one_hot(iota((lanes, total), 0) == lax.rem(atom, lanes))
        chunk = iota((chunks, total), 0) == lax.div(atom, lanes)
        owner.append(jnp.sum(jnp.where(chunk, dot(owner_of, hit), 0.0), axis=0, keepdims=True))
        within.append(jnp.sum(jnp.where(chunk, dot(within_of, hit), 0.0), axis=0, keepdims=True))
        key_row.append(group_row * groups + owner[side])
        key_column.append(column(key_row[side]))
    slot = [
        count((key_column[0] == key_row[0]) & before),
        count(key_column[0] == key_row[1]) + count((key_column[1] == key_row[1]) & before),
    ]
    sends = groups * SLOTS
    spots = (sends, total)
    dest = lax.div(iota(spots, 1), pairs) == lax.div(iota(spots, 0), SLOTS)
    turn = lax.rem(iota(spots, 0), SLOTS).astype(F32)
    entries = (2 * pairs, total)
    mine = iota(entries, 1) == me * pairs + lax.div(iota(entries, 0), 2)
    out, pick = 0.0, 0.0
    for side in range(2):
        chosen = dest & (slot[side] == turn) & (owner[side] == me.astype(F32))
        stored_at = column(within[side]).astype(jnp.int32) == iota((total, stored), 1)
        out += dot(one_hot(chosen), one_hot(stored_at))
        place = column(owner[side] * SLOTS + slot[side]).astype(jnp.int32)
        arrives = place == iota((total, sends), 1)
        local = mine & (lax.rem(iota(entries, 0), 2) == side)
        pick += dot(one_hot(local), one_hot(arrives))
    pick_ref[...] = pick.astype(BF16)
    local_aux, all_aux = metric_ref.shape[1:]
    twice = (2 * pairs, pairs)
    owns = lax.div(iota(twice, 0), 2) == iota(twice, 1)
    term = lax.rem(iota(twice, 0), 2)
    for q in range(local_aux):
        high, low = split_two(metric_ref[:, q, :] * SHRINK)
        both = dot(one_hot(owns & (term == 0)), high) + dot(one_hot(owns & (term == 1)), low)
        both = dot(both.astype(BF16), order_ref[...]).astype(BF16)
        terms_ref[:, q * all_aux : (q + 1) * all_aux] = both
    leaving = dot(out.astype(BF16), rows_ref[...]).astype(BF16)
    leaving_ref[...] = leaving.reshape(leaving_ref.shape)


def message_kernel(arrived_ref, pick_ref, metric_ref, density_ref, layout_ref, message_ref, block_ref):
    pairs = metric_ref.shape[0] // 2
    chips = message_ref.shape[0]
    arrived = arrived_ref[...].reshape(pick_ref.shape[1], arrived_ref.shape[2])
    rows = dot(pick_ref[...], arrived).astype(BF16)
    rows = jnp.concatenate([rows, metric_ref[...]], axis=1).reshape(pairs, 2, -1)
    empty = jnp.zeros((COLUMNS - pairs,) + rows.shape[1:], BF16)
    for line in range(0, chips, COLUMNS):
        message_ref[line : line + pairs] = rows
        message_ref[line + pairs : line + COLUMNS] = empty
    mine = lax.axis_index("row") * ACROSS + lax.axis_index("across")
    mine = iota((pairs, 1), 0) == jnp.minimum(mine, pairs - 1)
    block = jnp.sum(jnp.where(mine, density_ref[...].astype(F32), 0.0), axis=0, keepdims=True)
    segment, spread = layout_ref[0], layout_ref[1]
    block_ref[...] = dot_lanes((block * segment.astype(F32)).astype(BF16), spread).astype(BF16)


def exchange_kernel(given_ref, block_ref, layout_ref, out_ref):
    count = given_ref.shape[0]
    half = count // 2
    row, column = iota((count, count), 0), iota((count, count), 1)
    picked = jnp.where(row < half, 2 * row, 2 * (row - half) + 1) == column
    given = dot(picked.astype(BF16), given_ref[...]).astype(BF16)

    def stacked(part, start, width):
        part = part[:, start : start + LOCAL_AUX * width]
        return jnp.concatenate([part[:, q * width : (q + 1) * width] for q in range(LOCAL_AUX)], 0)

    first, second = stacked(given[:half], 0, BLOCK), stacked(given[half:], 0, BLOCK)
    terms = LOCAL_AUX * BLOCK
    high, low = stacked(given[:half], terms, count), stacked(given[half:], terms, count)
    largest = jnp.max(jnp.abs(high.astype(F32)), axis=0, keepdims=True)
    largest = jnp.maximum(jnp.max(largest, axis=1, keepdims=True), FLOOR)
    mixed = dot(high, second) + dot(low, second)
    high, low = split_two(mixed * (1.0 / largest))
    first = jnp.concatenate([first, first], 0).T
    mixed = jnp.concatenate([high, low], 0)
    segment, spread = layout_ref[0], layout_ref[1]
    weight = dot(block_ref[...], spread)[None]
    tops = []
    for m in range(0, NB, STEP):
        gram = dot(first[m * NB : (m + STEP) * NB], mixed)
        tops.append(jnp.sum(gram.reshape(STEP, NB, BLOCK) * weight, axis=1))
    top = jnp.concatenate(tops, 0)
    high, low = split_two(top)
    high, low = split_two(dot_lanes(high, segment) + dot_lanes(low, segment))
    flat = (dot(high, spread) + dot(low, spread)) * segment.astype(F32)
    flat = jnp.sum(flat, axis=0, keepdims=True) * largest * (1.0 / SHRINK)
    out_ref[...] = jnp.broadcast_to(flat[None], out_ref.shape)


def shards(coefficients, density, metric, pair_atoms, home_row):
    groups = lax.axis_size("atoms")
    columns = lax.axis_size(COLUMN_AXES)
    chips = lax.axis_size(CHIP_AXES)
    cores = lax.axis_size("core")
    width = coefficients.shape[1]
    pairs = density.shape[0]
    entries = 2 * pairs
    local_aux = width // BLOCK
    all_aux = chips * cores * local_aux

    in_vmem = pl.BlockSpec(memory_space=pltpu.VMEM)
    layout, order = pl.pallas_call(
        layout_kernel,
        out_specs=[in_vmem] * 2,
        out_shape=[
            jax.ShapeDtypeStruct((2, NB, BLOCK), BF16),
            jax.ShapeDtypeStruct((all_aux, all_aux), BF16),
        ],
        compiler_params=SMALL,
        cost_estimate=pl.CostEstimate(flops=FLOPS, bytes_accessed=BYTES, transcendentals=0),
    )()
    sources = [pair_atoms.T, home_row.reshape(-1, LANES), metric, order, coefficients]
    leaving, pick, terms = pl.pallas_call(
        leaving_kernel,
        in_specs=[in_vmem] * 5,
        out_specs=[in_vmem] * 3,
        out_shape=[
            jax.ShapeDtypeStruct((groups, SLOTS, width), BF16),
            jax.ShapeDtypeStruct((entries, groups * SLOTS), BF16),
            jax.ShapeDtypeStruct((entries, local_aux * all_aux), BF16),
        ],
        compiler_params=SMALL,
    )(*sources)
    arrived = lax.all_to_all(leaving, "atoms", 0, 0)

    message, block = pl.pallas_call(
        message_kernel,
        in_specs=[in_vmem] * 5,
        out_specs=[in_vmem] * 2,
        out_shape=[
            jax.ShapeDtypeStruct((chips, 2, width + local_aux * all_aux), BF16),
            jax.ShapeDtypeStruct((NB, NB), BF16),
        ],
        compiler_params=SMALL,
    )(arrived, pick, terms, density, layout)
    everyone = lax.all_to_all(message, CHIP_AXES, 0, 0)

    given = lax.all_gather(everyone, "core", axis=0, tiled=True)
    out = pl.pallas_call(
        exchange_kernel,
        out_shape=jax.ShapeDtypeStruct((columns, 1, BLOCK), F32),
        compiler_params=LARGE,
    )(given.reshape(chips * cores * 2, -1), block, layout)
    return lax.all_to_all(out, COLUMN_AXES, 0, 0)[:pairs, 0]


def solution(mesh):
    atoms, aux = mesh.devices.shape
    fine = mesh.devices.reshape(atoms, aux // (ROWS * ACROSS * CORES), ROWS, ACROSS, CORES)
    fine = Mesh(fine, ("atoms", "line", "row", "across", "core"))
    split = P("atoms", CHIP_AXES + ("core",))
    placed = (split, P("atoms", None), split, P(), P())
    return jax.shard_map(
        shards, mesh=fine, in_specs=placed, out_specs=P("atoms", None), check_vma=False
    )
```

```python
import jax
import jax.numpy as jnp
from jax import lax
from jax.experimental import pallas as pl
from jax.experimental.pallas import tpu as pltpu
from jax.sharding import Mesh, PartitionSpec as P

NB = 24
BLOCK = NB * NB
SLOTS = 2
ROWS, ACROSS, CORES = 2, 4, 2
COLUMNS = ROWS * ACROSS
LANES = 128
LOCAL_AUX = 2
STEP = 8
SHRINK, FLOOR = 2.0**-10, 1e-30
FLOPS, BYTES = 10**9, 10**6
COLUMN_AXES = ("row", "across")
CHIP_AXES = ("line",) + COLUMN_AXES
BF16 = jnp.bfloat16
F32 = jnp.float32
SMALL = pltpu.CompilerParams(vmem_limit_bytes=4 * 2**20)
LARGE = pltpu.CompilerParams(vmem_limit_bytes=16 * 2**20)


def split_two(x):
    high = x.astype(BF16)
    return high, (x - high.astype(F32)).astype(BF16)


def dot(a, b):
    return jnp.dot(a, b, preferred_element_type=F32)


def dot_lanes(a, b):
    return lax.dot_general(a, b, (((1,), (1,)), ((), ())), preferred_element_type=F32)


def iota(shape, dim):
    return lax.broadcasted_iota(jnp.int32, shape, dim)


def one_hot(condition):
    return condition.astype(F32).astype(BF16)


def layout_kernel(layout_ref, order_ref):
    place = iota((1, BLOCK), 1)
    major = lax.div(place, NB)
    index = iota((NB, BLOCK), 0)
    layout_ref[0] = one_hot(index == major)
    layout_ref[1] = one_hot(index == place - major * NB)
    square = order_ref.shape
    chips = square[0] // (CORES * LOCAL_AUX)
    function = iota((square[0], 1), 0)
    core = lax.rem(lax.div(function, LOCAL_AUX), CORES)
    target = lax.rem(function, LOCAL_AUX) * CORES + core
    target = target * chips + lax.div(function, CORES * LOCAL_AUX)
    order_ref[...] = one_hot(target == iota(square, 1))


def leaving_kernel(atoms_ref, home_ref, metric_ref, order_ref, rows_ref, leaving_ref, pick_ref, terms_ref):
    me = lax.axis_index("atoms")
    groups = leaving_ref.shape[0]
    stored = rows_ref.shape[0]
    chunks, lanes = home_ref.shape
    total = atoms_ref.shape[1]
    pairs = total // groups
    home = home_ref[...]
    owner_of = lax.div(home, stored).astype(F32).astype(BF16)
    within_of = lax.rem(home, stored).astype(F32).astype(BF16)
    square = (total, total)
    same = iota(square, 0) == iota(square, 1)
    before = iota(square, 0) < iota(square, 1)

    def column(x):
        return jnp.sum(jnp.where(same, x, 0.0), axis=1, keepdims=True)

    def count(condition):
        return jnp.sum(jnp.where(condition, 1.0, 0.0), axis=0, keepdims=True)

    group_row = lax.div(iota((1, total), 1), pairs).astype(F32)
    owner, within, key_row, key_column = [], [], [], []
    for side in range(2):
        atom = atoms_ref[side : side + 1, :]
        hit = one_hot(iota((lanes, total), 0) == lax.rem(atom, lanes))
        chunk = iota((chunks, total), 0) == lax.div(atom, lanes)
        owner.append(jnp.sum(jnp.where(chunk, dot(owner_of, hit), 0.0), axis=0, keepdims=True))
        within.append(jnp.sum(jnp.where(chunk, dot(within_of, hit), 0.0), axis=0, keepdims=True))
        key_row.append(group_row * groups + owner[side])
        key_column.append(column(key_row[side]))
    slot = [
        count((key_column[0] == key_row[0]) & before),
        count(key_column[0] == key_row[1]) + count((key_column[1] == key_row[1]) & before),
    ]
    sends = groups * SLOTS
    spots = (sends, total)
    dest = lax.div(iota(spots, 1), pairs) == lax.div(iota(spots, 0), SLOTS)
    turn = lax.rem(iota(spots, 0), SLOTS).astype(F32)
    entries = (2 * pairs, total)
    mine = iota(entries, 1) == me * pairs + lax.div(iota(entries, 0), 2)
    out, pick = 0.0, 0.0
    for side in range(2):
        chosen = dest & (slot[side] == turn) & (owner[side] == me.astype(F32))
        stored_at = column(within[side]).astype(jnp.int32) == iota((total, stored), 1)
        out += dot(one_hot(chosen), one_hot(stored_at))
        place = column(owner[side] * SLOTS + slot[side]).astype(jnp.int32)
        arrives = place == iota((total, sends), 1)
        local = mine & (lax.rem(iota(entries, 0), 2) == side)
        pick += dot(one_hot(local), one_hot(arrives))
    pick_ref[...] = pick.astype(BF16)
    local_aux, all_aux = metric_ref.shape[1:]
    twice = (2 * pairs, pairs)
    owns = lax.div(iota(twice, 0), 2) == iota(twice, 1)
    term = lax.rem(iota(twice, 0), 2)
    for q in range(local_aux):
        high, low = split_two(metric_ref[:, q, :] * SHRINK)
        both = dot(one_hot(owns & (term == 0)), high) + dot(one_hot(owns & (term == 1)), low)
        both = dot(both.astype(BF16), order_ref[...]).astype(BF16)
        terms_ref[:, q * all_aux : (q + 1) * all_aux] = both
    leaving = dot(out.astype(BF16), rows_ref[...]).astype(BF16)
    leaving_ref[...] = leaving.reshape(leaving_ref.shape)


def message_kernel(arrived_ref, pick_ref, metric_ref, density_ref, layout_ref, message_ref, block_ref):
    pairs = metric_ref.shape[0] // 2
    chips = message_ref.shape[0]
    arrived = arrived_ref[...].reshape(pick_ref.shape[1], arrived_ref.shape[2])
    rows = dot(pick_ref[...], arrived).astype(BF16)
    rows = jnp.concatenate([rows, metric_ref[...]], axis=1).reshape(pairs, 2, -1)
    empty = jnp.zeros((COLUMNS - pairs,) + rows.shape[1:], BF16)
    for line in range(0, chips, COLUMNS):
        message_ref[line : line + pairs] = rows
        message_ref[line + pairs : line + COLUMNS] = empty
    mine = lax.axis_index("row") * ACROSS + lax.axis_index("across")
    mine = iota((pairs, 1), 0) == jnp.minimum(mine, pairs - 1)
    block = jnp.sum(jnp.where(mine, density_ref[...].astype(F32), 0.0), axis=0, keepdims=True)
    segment, spread = layout_ref[0], layout_ref[1]
    block_ref[...] = dot_lanes((block * segment.astype(F32)).astype(BF16), spread).astype(BF16)


def exchange_kernel(given_ref, block_ref, layout_ref, out_ref):
    half = given_ref.shape[0]
    count = 2 * half
    row, column = iota((count, count), 0), iota((count, count), 1)
    picked = jnp.where(row < half, 2 * row, 2 * (row - half) + 1) == column
    given = given_ref[...].reshape(count, given_ref.shape[2])
    given = dot(picked.astype(BF16), given).astype(BF16)

    def stacked(part, start, width):
        part = part[:, start : start + LOCAL_AUX * width]
        return jnp.concatenate([part[:, q * width : (q + 1) * width] for q in range(LOCAL_AUX)], 0)

    first, second = stacked(given[:half], 0, BLOCK), stacked(given[half:], 0, BLOCK)
    terms = LOCAL_AUX * BLOCK
    high, low = stacked(given[:half], terms, count), stacked(given[half:], terms, count)
    largest = jnp.max(jnp.abs(high.astype(F32)), axis=0, keepdims=True)
    largest = jnp.maximum(jnp.max(largest, axis=1, keepdims=True), FLOOR)
    mixed = dot(high, second) + dot(low, second)
    high, low = split_two(mixed * (1.0 / largest))
    first = jnp.concatenate([first, first], 0).T
    mixed = jnp.concatenate([high, low], 0)
    segment, spread = layout_ref[0], layout_ref[1]
    weight = dot(block_ref[...], spread)[None]
    tops = []
    for m in range(0, NB, STEP):
        gram = dot(first[m * NB : (m + STEP) * NB], mixed)
        tops.append(jnp.sum(gram.reshape(STEP, NB, BLOCK) * weight, axis=1))
    top = jnp.concatenate(tops, 0)
    high, low = split_two(top)
    high, low = split_two(dot_lanes(high, segment) + dot_lanes(low, segment))
    flat = (dot(high, spread) + dot(low, spread)) * segment.astype(F32)
    flat = jnp.sum(flat, axis=0, keepdims=True) * largest * (1.0 / SHRINK)
    out_ref[...] = jnp.broadcast_to(flat[None], out_ref.shape)


def shards(coefficients, density, metric, pair_atoms, home_row):
    groups = lax.axis_size("atoms")
    columns = lax.axis_size(COLUMN_AXES)
    chips = lax.axis_size(CHIP_AXES)
    cores = lax.axis_size("core")
    width = coefficients.shape[1]
    pairs = density.shape[0]
    entries = 2 * pairs
    local_aux = width // BLOCK
    all_aux = chips * cores * local_aux

    in_vmem = pl.BlockSpec(memory_space=pltpu.VMEM)
    layout, order = pl.pallas_call(
        layout_kernel,
        out_specs=[in_vmem] * 2,
        out_shape=[
            jax.ShapeDtypeStruct((2, NB, BLOCK), BF16),
            jax.ShapeDtypeStruct((all_aux, all_aux), BF16),
        ],
        compiler_params=SMALL,
        cost_estimate=pl.CostEstimate(flops=FLOPS, bytes_accessed=BYTES, transcendentals=0),
    )()
    sources = [pair_atoms.T, home_row.reshape(-1, LANES), metric, order, coefficients]
    leaving, pick, terms = pl.pallas_call(
        leaving_kernel,
        in_specs=[in_vmem] * 5,
        out_specs=[in_vmem] * 3,
        out_shape=[
            jax.ShapeDtypeStruct((groups, SLOTS, width), BF16),
            jax.ShapeDtypeStruct((entries, groups * SLOTS), BF16),
            jax.ShapeDtypeStruct((entries, local_aux * all_aux), BF16),
        ],
        compiler_params=SMALL,
    )(*sources)
    arrived = lax.all_to_all(leaving, "atoms", 0, 0)

    message, block = pl.pallas_call(
        message_kernel,
        in_specs=[in_vmem] * 5,
        out_specs=[in_vmem] * 2,
        out_shape=[
            jax.ShapeDtypeStruct((chips, 2, width + local_aux * all_aux), BF16),
            jax.ShapeDtypeStruct((NB, NB), BF16),
        ],
        compiler_params=SMALL,
    )(arrived, pick, terms, density, layout)
    everyone = lax.all_to_all(message, CHIP_AXES, 0, 0)

    given = lax.all_gather(everyone, "core", axis=0, tiled=True)
    out = pl.pallas_call(
        exchange_kernel,
        out_shape=jax.ShapeDtypeStruct((columns, 1, BLOCK), F32),
        compiler_params=LARGE,
    )(given, block, layout)
    return lax.all_to_all(out, COLUMN_AXES, 0, 0)[:pairs, 0]


def solution(mesh):
    atoms, aux = mesh.devices.shape
    fine = mesh.devices.reshape(atoms, aux // (ROWS * ACROSS * CORES), ROWS, ACROSS, CORES)
    fine = Mesh(fine, ("atoms", "line", "row", "across", "core"))
    split = P("atoms", CHIP_AXES + ("core",))
    placed = (split, P("atoms", None), split, P(), P())
    return jax.shard_map(
        shards, mesh=fine, in_specs=placed, out_specs=P("atoms", None), check_vma=False
    )
```

```python
import jax
import jax.numpy as jnp
from jax import lax
from jax.experimental import pallas as pl
from jax.experimental.pallas import tpu as pltpu
from jax.sharding import Mesh, PartitionSpec as P

NB = 24
BLOCK = NB * NB
SLOTS = 2
ROWS, ACROSS, CORES = 2, 4, 2
COLUMNS = ROWS * ACROSS
LANES = 128
LOCAL_AUX = 2
STEP = 12
SHRINK, FLOOR = 2.0**-10, 1e-30
FLOPS, BYTES = 10**9, 10**6
COLUMN_AXES = ("row", "across")
CHIP_AXES = ("line",) + COLUMN_AXES
BF16 = jnp.bfloat16
F32 = jnp.float32
SMALL = pltpu.CompilerParams(vmem_limit_bytes=4 * 2**20)
LARGE = pltpu.CompilerParams(vmem_limit_bytes=16 * 2**20)


def split_two(x):
    high = x.astype(BF16)
    return high, (x - high.astype(F32)).astype(BF16)


def dot(a, b):
    return jnp.dot(a, b, preferred_element_type=F32)


def dot_lanes(a, b):
    return lax.dot_general(a, b, (((1,), (1,)), ((), ())), preferred_element_type=F32)


def iota(shape, dim):
    return lax.broadcasted_iota(jnp.int32, shape, dim)


def one_hot(condition):
    return condition.astype(F32).astype(BF16)


def layout_kernel(layout_ref, order_ref):
    place = iota((1, BLOCK), 1)
    major = lax.div(place, NB)
    index = iota((NB, BLOCK), 0)
    layout_ref[0] = one_hot(index == major)
    layout_ref[1] = one_hot(index == place - major * NB)
    square = order_ref.shape
    chips = square[0] // (CORES * LOCAL_AUX)
    function = iota((square[0], 1), 0)
    core = lax.rem(lax.div(function, LOCAL_AUX), CORES)
    target = lax.rem(function, LOCAL_AUX) * CORES + core
    target = target * chips + lax.div(function, CORES * LOCAL_AUX)
    order_ref[...] = one_hot(target == iota(square, 1))


def leaving_kernel(atoms_ref, home_ref, metric_ref, order_ref, rows_ref, leaving_ref, pick_ref, terms_ref):
    me = lax.axis_index("atoms")
    groups = leaving_ref.shape[0]
    stored = rows_ref.shape[0]
    chunks, lanes = home_ref.shape
    total = atoms_ref.shape[1]
    pairs = total // groups
    home = home_ref[...]
    owner_of = lax.div(home, stored).astype(F32).astype(BF16)
    within_of = lax.rem(home, stored).astype(F32).astype(BF16)
    square = (total, total)
    same = iota(square, 0) == iota(square, 1)
    before = iota(square, 0) < iota(square, 1)

    def column(x):
        return jnp.sum(jnp.where(same, x, 0.0), axis=1, keepdims=True)

    def count(condition):
        return jnp.sum(jnp.where(condition, 1.0, 0.0), axis=0, keepdims=True)

    group_row = lax.div(iota((1, total), 1), pairs).astype(F32)
    owner, within, key_row, key_column = [], [], [], []
    for side in range(2):
        atom = atoms_ref[side : side + 1, :]
        hit = one_hot(iota((lanes, total), 0) == lax.rem(atom, lanes))
        chunk = iota((chunks, total), 0) == lax.div(atom, lanes)
        owner.append(jnp.sum(jnp.where(chunk, dot(owner_of, hit), 0.0), axis=0, keepdims=True))
        within.append(jnp.sum(jnp.where(chunk, dot(within_of, hit), 0.0), axis=0, keepdims=True))
        key_row.append(group_row * groups + owner[side])
        key_column.append(column(key_row[side]))
    slot = [
        count((key_column[0] == key_row[0]) & before),
        count(key_column[0] == key_row[1]) + count((key_column[1] == key_row[1]) & before),
    ]
    sends = groups * SLOTS
    spots = (sends, total)
    dest = lax.div(iota(spots, 1), pairs) == lax.div(iota(spots, 0), SLOTS)
    turn = lax.rem(iota(spots, 0), SLOTS).astype(F32)
    entries = (2 * pairs, total)
    mine = iota(entries, 1) == me * pairs + lax.div(iota(entries, 0), 2)
    out, pick = 0.0, 0.0
    for side in range(2):
        chosen = dest & (slot[side] == turn) & (owner[side] == me.astype(F32))
        stored_at = column(within[side]).astype(jnp.int32) == iota((total, stored), 1)
        out += dot(one_hot(chosen), one_hot(stored_at))
        place = column(owner[side] * SLOTS + slot[side]).astype(jnp.int32)
        arrives = place == iota((total, sends), 1)
        local = mine & (lax.rem(iota(entries, 0), 2) == side)
        pick += dot(one_hot(local), one_hot(arrives))
    pick_ref[...] = pick.astype(BF16)
    local_aux, all_aux = metric_ref.shape[1:]
    twice = (2 * pairs, pairs)
    owns = lax.div(iota(twice, 0), 2) == iota(twice, 1)
    term = lax.rem(iota(twice, 0), 2)
    for q in range(local_aux):
        high, low = split_two(metric_ref[:, q, :] * SHRINK)
        both = dot(one_hot(owns & (term == 0)), high) + dot(one_hot(owns & (term == 1)), low)
        both = dot(both.astype(BF16), order_ref[...]).astype(BF16)
        terms_ref[:, q * all_aux : (q + 1) * all_aux] = both
    leaving = dot(out.astype(BF16), rows_ref[...]).astype(BF16)
    leaving_ref[...] = leaving.reshape(leaving_ref.shape)


def message_kernel(arrived_ref, pick_ref, metric_ref, density_ref, layout_ref, message_ref, block_ref):
    pairs = metric_ref.shape[0] // 2
    chips = message_ref.shape[0]
    arrived = arrived_ref[...].reshape(pick_ref.shape[1], arrived_ref.shape[2])
    rows = dot(pick_ref[...], arrived).astype(BF16)
    rows = jnp.concatenate([rows, metric_ref[...]], axis=1).reshape(pairs, 2, -1)
    empty = jnp.zeros((COLUMNS - pairs,) + rows.shape[1:], BF16)
    for line in range(0, chips, COLUMNS):
        message_ref[line : line + pairs] = rows
        message_ref[line + pairs : line + COLUMNS] = empty
    mine = lax.axis_index("row") * ACROSS + lax.axis_index("across")
    mine = iota((pairs, 1), 0) == jnp.minimum(mine, pairs - 1)
    block = jnp.sum(jnp.where(mine, density_ref[...].astype(F32), 0.0), axis=0, keepdims=True)
    segment, spread = layout_ref[0], layout_ref[1]
    block_ref[...] = dot_lanes((block * segment.astype(F32)).astype(BF16), spread).astype(BF16)


def exchange_kernel(given_ref, block_ref, layout_ref, out_ref):
    half = given_ref.shape[0]
    count = 2 * half
    row, column = iota((count, count), 0), iota((count, count), 1)
    picked = jnp.where(row < half, 2 * row, 2 * (row - half) + 1) == column
    given = given_ref[...].reshape(count, given_ref.shape[2])
    given = dot(picked.astype(BF16), given).astype(BF16)

    def stacked(part, start, width):
        part = part[:, start : start + LOCAL_AUX * width]
        return jnp.concatenate([part[:, q * width : (q + 1) * width] for q in range(LOCAL_AUX)], 0)

    first, second = stacked(given[:half], 0, BLOCK), stacked(given[half:], 0, BLOCK)
    terms = LOCAL_AUX * BLOCK
    high, low = stacked(given[:half], terms, count), stacked(given[half:], terms, count)
    largest = jnp.max(jnp.abs(high.astype(F32)), axis=0, keepdims=True)
    largest = jnp.maximum(jnp.max(largest, axis=1, keepdims=True), FLOOR)
    terms = jnp.concatenate([high, low], 1)
    mixed = dot(terms, jnp.concatenate([second, second], 0))
    high, low = split_two(mixed * (1.0 / largest))
    first = jnp.concatenate([first, first], 0).T
    mixed = jnp.concatenate([high, low], 0)
    segment, spread = layout_ref[0], layout_ref[1]
    weight = dot(block_ref[...], spread)[None]
    tops = []
    for m in range(0, NB, STEP):
        gram = dot(first[m * NB : (m + STEP) * NB], mixed)
        tops.append(jnp.sum(gram.reshape(STEP, NB, BLOCK) * weight, axis=1))
    top = jnp.concatenate(tops, 0)
    high, low = split_two(top)
    high, low = split_two(dot_lanes(high, segment) + dot_lanes(low, segment))
    flat = (dot(high, spread) + dot(low, spread)) * segment.astype(F32)
    flat = jnp.sum(flat, axis=0, keepdims=True) * largest * (1.0 / SHRINK)
    out_ref[...] = jnp.broadcast_to(flat[None], out_ref.shape)


def shards(coefficients, density, metric, pair_atoms, home_row):
    groups = lax.axis_size("atoms")
    columns = lax.axis_size(COLUMN_AXES)
    chips = lax.axis_size(CHIP_AXES)
    cores = lax.axis_size("core")
    width = coefficients.shape[1]
    pairs = density.shape[0]
    entries = 2 * pairs
    local_aux = width // BLOCK
    all_aux = chips * cores * local_aux

    in_vmem = pl.BlockSpec(memory_space=pltpu.VMEM)
    layout, order = pl.pallas_call(
        layout_kernel,
        out_specs=[in_vmem] * 2,
        out_shape=[
            jax.ShapeDtypeStruct((2, NB, BLOCK), BF16),
            jax.ShapeDtypeStruct((all_aux, all_aux), BF16),
        ],
        compiler_params=SMALL,
        cost_estimate=pl.CostEstimate(flops=FLOPS, bytes_accessed=BYTES, transcendentals=0),
    )()
    sources = [pair_atoms.T, home_row.reshape(-1, LANES), metric, order, coefficients]
    leaving, pick, terms = pl.pallas_call(
        leaving_kernel,
        in_specs=[in_vmem] * 5,
        out_specs=[in_vmem] * 3,
        out_shape=[
            jax.ShapeDtypeStruct((groups, SLOTS, width), BF16),
            jax.ShapeDtypeStruct((entries, groups * SLOTS), BF16),
            jax.ShapeDtypeStruct((entries, local_aux * all_aux), BF16),
        ],
        compiler_params=SMALL,
    )(*sources)
    arrived = lax.all_to_all(leaving, "atoms", 0, 0)

    message, block = pl.pallas_call(
        message_kernel,
        in_specs=[in_vmem] * 5,
        out_specs=[in_vmem] * 2,
        out_shape=[
            jax.ShapeDtypeStruct((chips, 2, width + local_aux * all_aux), BF16),
            jax.ShapeDtypeStruct((NB, NB), BF16),
        ],
        compiler_params=SMALL,
    )(arrived, pick, terms, density, layout)
    everyone = lax.all_to_all(message, CHIP_AXES, 0, 0)

    given = lax.all_gather(everyone, "core", axis=0, tiled=True)
    out = pl.pallas_call(
        exchange_kernel,
        out_shape=jax.ShapeDtypeStruct((columns, 1, BLOCK), F32),
        compiler_params=LARGE,
    )(given, block, layout)
    return lax.all_to_all(out, COLUMN_AXES, 0, 0)[:pairs, 0]


def solution(mesh):
    atoms, aux = mesh.devices.shape
    fine = mesh.devices.reshape(atoms, aux // (ROWS * ACROSS * CORES), ROWS, ACROSS, CORES)
    fine = Mesh(fine, ("atoms", "line", "row", "across", "core"))
    split = P("atoms", CHIP_AXES + ("core",))
    placed = (split, P("atoms", None), split, P(), P())
    return jax.shard_map(
        shards, mesh=fine, in_specs=placed, out_specs=P("atoms", None), check_vma=False
    )
```

```python
import jax
import jax.numpy as jnp
from jax import lax
from jax.experimental import pallas as pl
from jax.experimental.pallas import tpu as pltpu
from jax.sharding import Mesh, PartitionSpec as P

NB = 24
BLOCK = NB * NB
SLOTS = 2
ROWS, ACROSS, CORES = 2, 4, 2
COLUMNS = ROWS * ACROSS
LANES = 128
LOCAL_AUX = 2
STEP = 8
SHRINK, FLOOR = 2.0**-10, 1e-30
FLOPS, BYTES = 10**9, 10**6
COLUMN_AXES = ("row", "across")
CHIP_AXES = ("line",) + COLUMN_AXES
BF16 = jnp.bfloat16
F32 = jnp.float32
SMALL = pltpu.CompilerParams(vmem_limit_bytes=4 * 2**20)
LARGE = pltpu.CompilerParams(vmem_limit_bytes=16 * 2**20)


def split_two(x):
    high = x.astype(BF16)
    return high, (x - high.astype(F32)).astype(BF16)


def dot(a, b):
    return jnp.dot(a, b, preferred_element_type=F32)


def dot_lanes(a, b):
    return lax.dot_general(a, b, (((1,), (1,)), ((), ())), preferred_element_type=F32)


def iota(shape, dim):
    return lax.broadcasted_iota(jnp.int32, shape, dim)


def one_hot(condition):
    return condition.astype(F32).astype(BF16)


def layout_kernel(layout_ref, order_ref):
    place = iota((1, BLOCK), 1)
    major = lax.div(place, NB)
    index = iota((NB, BLOCK), 0)
    layout_ref[0] = one_hot(index == major)
    layout_ref[1] = one_hot(index == place - major * NB)
    square = order_ref.shape
    chips = square[0] // (CORES * LOCAL_AUX)
    function = iota((square[0], 1), 0)
    core = lax.rem(lax.div(function, LOCAL_AUX), CORES)
    target = lax.rem(function, LOCAL_AUX) * CORES + core
    target = target * chips + lax.div(function, CORES * LOCAL_AUX)
    order_ref[...] = one_hot(target == iota(square, 1))


def leaving_kernel(atoms_ref, home_ref, metric_ref, order_ref, rows_ref, leaving_ref, pick_ref, terms_ref):
    me = lax.axis_index("atoms")
    groups = leaving_ref.shape[0]
    stored = rows_ref.shape[0]
    chunks, lanes = home_ref.shape
    total = atoms_ref.shape[1]
    pairs = total // groups
    home = home_ref[...]
    owner_of = lax.div(home, stored).astype(F32).astype(BF16)
    within_of = lax.rem(home, stored).astype(F32).astype(BF16)
    square = (total, total)
    same = iota(square, 0) == iota(square, 1)
    before = iota(square, 0) < iota(square, 1)

    def column(x):
        return jnp.sum(jnp.where(same, x, 0.0), axis=1, keepdims=True)

    def count(condition):
        return jnp.sum(jnp.where(condition, 1.0, 0.0), axis=0, keepdims=True)

    group_row = lax.div(iota((1, total), 1), pairs).astype(F32)
    owner, within, key_row, key_column = [], [], [], []
    for side in range(2):
        atom = atoms_ref[side : side + 1, :]
        hit = one_hot(iota((lanes, total), 0) == lax.rem(atom, lanes))
        chunk = iota((chunks, total), 0) == lax.div(atom, lanes)
        owner.append(jnp.sum(jnp.where(chunk, dot(owner_of, hit), 0.0), axis=0, keepdims=True))
        within.append(jnp.sum(jnp.where(chunk, dot(within_of, hit), 0.0), axis=0, keepdims=True))
        key_row.append(group_row * groups + owner[side])
        key_column.append(column(key_row[side]))
    slot = [
        count((key_column[0] == key_row[0]) & before),
        count(key_column[0] == key_row[1]) + count((key_column[1] == key_row[1]) & before),
    ]
    sends = groups * SLOTS
    spots = (sends, total)
    dest = lax.div(iota(spots, 1), pairs) == lax.div(iota(spots, 0), SLOTS)
    turn = lax.rem(iota(spots, 0), SLOTS).astype(F32)
    entries = (2 * pairs, total)
    mine = iota(entries, 1) == me * pairs + lax.div(iota(entries, 0), 2)
    out, pick = 0.0, 0.0
    for side in range(2):
        chosen = dest & (slot[side] == turn) & (owner[side] == me.astype(F32))
        stored_at = column(within[side]).astype(jnp.int32) == iota((total, stored), 1)
        out += dot(one_hot(chosen), one_hot(stored_at))
        place = column(owner[side] * SLOTS + slot[side]).astype(jnp.int32)
        arrives = place == iota((total, sends), 1)
        local = mine & (lax.rem(iota(entries, 0), 2) == side)
        pick += dot(one_hot(local), one_hot(arrives))
    pick_ref[...] = pick.astype(BF16)
    local_aux, all_aux = metric_ref.shape[1:]
    twice = (2 * pairs, pairs)
    owns = lax.div(iota(twice, 0), 2) == iota(twice, 1)
    term = lax.rem(iota(twice, 0), 2)
    for q in range(local_aux):
        high, low = split_two(metric_ref[:, q, :] * SHRINK)
        both = dot(one_hot(owns & (term == 0)), high) + dot(one_hot(owns & (term == 1)), low)
        both = dot(both.astype(BF16), order_ref[...]).astype(BF16)
        terms_ref[:, q * all_aux : (q + 1) * all_aux] = both
    leaving = dot(out.astype(BF16), rows_ref[...]).astype(BF16)
    leaving_ref[...] = leaving.reshape(leaving_ref.shape)


def message_kernel(arrived_ref, pick_ref, metric_ref, density_ref, layout_ref, message_ref, block_ref):
    pairs = metric_ref.shape[0] // 2
    chips = message_ref.shape[0]
    arrived = arrived_ref[...].reshape(pick_ref.shape[1], arrived_ref.shape[2])
    rows = dot(pick_ref[...], arrived).astype(BF16)
    rows = jnp.concatenate([rows, metric_ref[...]], axis=1).reshape(pairs, 2, -1)
    empty = jnp.zeros((COLUMNS - pairs,) + rows.shape[1:], BF16)
    for line in range(0, chips, COLUMNS):
        message_ref[line : line + pairs] = rows
        message_ref[line + pairs : line + COLUMNS] = empty
    mine = lax.axis_index("row") * ACROSS + lax.axis_index("across")
    mine = iota((pairs, 1), 0) == jnp.minimum(mine, pairs - 1)
    block = jnp.sum(jnp.where(mine, density_ref[...].astype(F32), 0.0), axis=0, keepdims=True)
    segment, spread = layout_ref[0], layout_ref[1]
    block_ref[...] = dot_lanes((block * segment.astype(F32)).astype(BF16), spread).astype(BF16)


def exchange_kernel(given_ref, block_ref, layout_ref, out_ref):
    half = given_ref.shape[0]
    count = 2 * half
    row, column = iota((count, count), 0), iota((count, count), 1)
    picked = jnp.where(row < half, 2 * row, 2 * (row - half) + 1) == column
    given = given_ref[...].reshape(count, given_ref.shape[2])
    given = dot(picked.astype(BF16), given).astype(BF16)

    def stacked(part, start, width):
        part = part[:, start : start + LOCAL_AUX * width]
        return jnp.concatenate([part[:, q * width : (q + 1) * width] for q in range(LOCAL_AUX)], 0)

    first, second = stacked(given[:half], 0, BLOCK), stacked(given[half:], 0, BLOCK)
    terms = LOCAL_AUX * BLOCK
    high, low = stacked(given[:half], terms, count), stacked(given[half:], terms, count)
    largest = jnp.max(jnp.abs(high.astype(F32)), axis=0, keepdims=True)
    largest = jnp.maximum(jnp.max(largest, axis=1, keepdims=True), FLOOR)
    terms = jnp.concatenate([high, low], 1)
    mixed = dot(terms, jnp.concatenate([second, second], 0))
    high, low = split_two(mixed * (1.0 / largest))
    first = jnp.concatenate([first, first], 0).T
    mixed = jnp.concatenate([high, low], 0)
    segment, spread = layout_ref[0], layout_ref[1]
    weight = dot(block_ref[...], spread)[None]
    tops = []
    for m in range(0, NB, STEP):
        gram = dot(first[m * NB : (m + STEP) * NB], mixed)
        tops.append(jnp.sum(gram.reshape(STEP, NB, BLOCK) * weight, axis=1))
    top = jnp.concatenate(tops, 0)
    high, low = split_two(top)
    high, low = split_two(dot_lanes(high, segment) + dot_lanes(low, segment))
    flat = (dot(high, spread) + dot(low, spread)) * segment.astype(F32)
    flat = jnp.sum(flat, axis=0, keepdims=True) * largest * (1.0 / SHRINK)
    out_ref[...] = jnp.broadcast_to(flat[None], out_ref.shape)


def shards(coefficients, density, metric, pair_atoms, home_row):
    groups = lax.axis_size("atoms")
    columns = lax.axis_size(COLUMN_AXES)
    chips = lax.axis_size(CHIP_AXES)
    cores = lax.axis_size("core")
    width = coefficients.shape[1]
    pairs = density.shape[0]
    entries = 2 * pairs
    local_aux = width // BLOCK
    all_aux = chips * cores * local_aux

    in_vmem = pl.BlockSpec(memory_space=pltpu.VMEM)
    layout, order = pl.pallas_call(
        layout_kernel,
        out_specs=[in_vmem] * 2,
        out_shape=[
            jax.ShapeDtypeStruct((2, NB, BLOCK), BF16),
            jax.ShapeDtypeStruct((all_aux, all_aux), BF16),
        ],
        compiler_params=SMALL,
        cost_estimate=pl.CostEstimate(flops=FLOPS, bytes_accessed=BYTES, transcendentals=0),
    )()
    sources = [pair_atoms.T, home_row.reshape(-1, LANES), metric, order, coefficients]
    leaving, pick, terms = pl.pallas_call(
        leaving_kernel,
        in_specs=[in_vmem] * 5,
        out_specs=[in_vmem] * 3,
        out_shape=[
            jax.ShapeDtypeStruct((groups, SLOTS, width), BF16),
            jax.ShapeDtypeStruct((entries, groups * SLOTS), BF16),
            jax.ShapeDtypeStruct((entries, local_aux * all_aux), BF16),
        ],
        compiler_params=SMALL,
    )(*sources)
    arrived = lax.all_to_all(leaving, "atoms", 0, 0)

    message, block = pl.pallas_call(
        message_kernel,
        in_specs=[in_vmem] * 5,
        out_specs=[in_vmem] * 2,
        out_shape=[
            jax.ShapeDtypeStruct((chips, 2, width + local_aux * all_aux), BF16),
            jax.ShapeDtypeStruct((NB, NB), BF16),
        ],
        compiler_params=SMALL,
    )(arrived, pick, terms, density, layout)
    everyone = lax.all_to_all(message, CHIP_AXES, 0, 0)

    given = lax.all_gather(everyone, "core", axis=0, tiled=True)
    out = pl.pallas_call(
        exchange_kernel,
        out_shape=jax.ShapeDtypeStruct((columns, 1, BLOCK), F32),
        compiler_params=LARGE,
    )(given, block, layout)
    return lax.all_to_all(out, COLUMN_AXES, 0, 0)[:pairs, 0]


def solution(mesh):
    atoms, aux = mesh.devices.shape
    fine = mesh.devices.reshape(atoms, aux // (ROWS * ACROSS * CORES), ROWS, ACROSS, CORES)
    fine = Mesh(fine, ("atoms", "line", "row", "across", "core"))
    split = P("atoms", CHIP_AXES + ("core",))
    placed = (split, P("atoms", None), split, P(), P())
    return jax.shard_map(
        shards, mesh=fine, in_specs=placed, out_specs=P("atoms", None), check_vma=False
    )
```
